256 devices in a mesh: gx: 32 (over y_lo, z, core), row: 8 (over y_hi, x).
Axes of the slice: x: 4, y: 4 (y_hi: 2, y_lo: 2; y = y_hi * 2 + y_lo), z: 8, core: 2. Of those that a mesh axis runs over, the one named last changes fastest.
Arguments:
- config_fields: float32 [32, 3, 128, 96, 128], P('row', None, 'gx'), may hold values from -6 to 6
- velocity: float32 [3, 128, 96, 128], P(None, 'gx'), may hold values from -0.4 to 3.1
- noise_keys: int32 [32, 2], P('row'), may hold values from 0 to 1048575
Outputs:
- config_out: float32 [32, 3, 128, 96, 128], P('row', None, 'gx')
- velocity_out: float32 [3, 128, 96, 128], P(None, 'gx')
The draws below stay inside these ranges and needn't reach their ends.
All inputs are finite; a program needn't handle non-finite values.
Results may differ from the reference program's by a relative error of at most 0.00017.
Values sent between devices are 32-bit elements; how exact they have to be, the bound alone decides.
No kernel may reach another device: no remote copies, remote signals or barrier semaphores. Data moves between devices by JAX's collectives and lax.ppermute only.
A program may use at most 128 MiB of HBM per device.

```python
import math
import jax
import jax.numpy as jnp
from jax import lax

NY = 96
NZ = 128
STEPS = 2
FIELDS = 32
NX = 128


def draw_velocity(key, part):
    xpos = (jnp.arange(NX, dtype=jnp.float32) + 0.5) / NX
    ypos = (jnp.arange(NY, dtype=jnp.float32) + 0.5) / NY
    profile = 4.0 * ypos * (1.0 - ypos)
    ramp = 0.3 + 0.6 * xpos
    spread = 0.3
    base = 1.5 * ramp[:, None, None] * profile[None, :, None] * jnp.ones((1, 1, NZ), jnp.float32)
    rough = jax.random.uniform(key, (3, NX, NY, NZ), jnp.float32, -spread, spread)
    stream = base + rough[0]
    return jnp.concatenate([stream[None], rough[1:]], axis=0).astype(jnp.float32)


def with_ends(values, rng, low, top_value):
    longest = values.shape.index(max(values.shape))
    spots = []
    for shift in (0, 1):
        where = [jax.random.randint(jax.random.fold_in(rng, axis), (), 0, length) for axis, length in enumerate(values.shape)]
        where[longest] = (where[longest] + shift) % values.shape[longest]
        spots.append(tuple(where))
    return values.at[spots[0]].set(low).at[spots[1]].set(top_value)


def shard_levels(own_key, dims, cuts, smallest, high):
    def one(dim, shards_of):
        heights = jax.random.uniform(jax.random.fold_in(jax.random.fold_in(own_key, 6), dim), (shards_of,), jnp.float32, smallest / len(cuts), high / len(cuts))
        return jnp.repeat(jnp.exp(heights), dims[dim] // shards_of).reshape((-1,) + (1,) * (len(dims) - dim - 1))

    factor_of = one(*cuts[0])
    for cut in cuts[1:]:
        factor_of = factor_of * one(*cut)
    return factor_of


def gaussian(rng, dims, deviation, bound, shards=(), kind=jnp.bfloat16):
    entries = deviation * jax.random.normal(rng, dims, jnp.float32)
    if shards:
        entries = entries * shard_levels(rng, dims, shards, -0.22, 0.18)
    return jnp.clip(entries, -bound, bound).astype(kind)


def setup_inputs(seed: int = 0) -> dict:
    key_list = jax.random.split(jax.random.key(seed), 4)
    config_fields = gaussian(key_list[0], (FIELDS, 3, NX, NY, NZ), 1.0, 6.0, ((0, 8), (2, 32)), jnp.float32)
    velocity = draw_velocity(jax.random.fold_in(key_list[3], 71), 0)
    noise_keys = with_ends(jax.random.randint(key_list[2], (FIELDS, STEPS), 0, 1048576), jax.random.fold_in(key_list[2], 1), 0, 1048575).astype(jnp.int32)
    return dict(config_fields=config_fields, velocity=velocity, noise_keys=noise_keys)


time_step = 0.05
viscosity = 0.5
stress_coef = 4.0
relax_time = 0.5
spring_limit = 10.0
spring_floor = 0.2
bulk_target = 1.0

def mix_bits(value):
    value = value ^ lax.shift_right_logical(value, jnp.int32(16))
    value = value * jnp.int32(73244475)
    value = value ^ lax.shift_right_logical(value, jnp.int32(16))
    value = value * jnp.int32(73244475)
    return value ^ lax.shift_right_logical(value, jnp.int32(16))

def gauss_noise(key, index):
    salted = mix_bits(key + jnp.int32(40503))
    first = mix_bits(index * 2 ^ salted)
    second = mix_bits(index * 2 + 1 ^ salted)
    mask = jnp.int32(16777215)
    upper = ((first & mask).astype(jnp.float32) + 0.5) / 16777216.0
    lower = ((second & mask).astype(jnp.float32) + 0.5) / 16777216.0
    return jnp.sqrt(-2.0 * jnp.log(upper)) * jnp.cos(6.283185307179586 * lower)

def cell_index(x_start, count, total_x, rows, depth):
    shape = (3, count, rows, depth)
    comp = lax.broadcasted_iota(jnp.int32, shape, 0)
    xpos = lax.broadcasted_iota(jnp.int32, shape, 1) + x_start
    ypos = lax.broadcasted_iota(jnp.int32, shape, 2)
    zpos = lax.broadcasted_iota(jnp.int32, shape, 3)
    return ((comp * total_x + xpos) * rows + ypos) * depth + zpos

def wrap_x(array):
    return jnp.concatenate([array[..., -1:, :, :], array, array[..., :1, :, :]], axis=-3)

def diff_x(extended):
    return 0.5 * (extended[..., 2:, :, :] - extended[..., :-2, :, :])

def diff_y(field):
    widths = [(0, 0)] * (field.ndim - 2) + [(1, 1), (0, 0)]
    padded = jnp.pad(field, widths)
    return 0.5 * (padded[..., 2:, :] - padded[..., :-2, :])

def diff_z(field):
    return 0.5 * (jnp.roll(field, -1, -1) - jnp.roll(field, 1, -1))

def spring_factor(extended):
    length = lax.optimization_barrier(jnp.sum(extended * extended, axis=-4))
    return 1.0 / jnp.maximum(1.0 - length / spring_limit, spring_floor)

def divergence(stress):
    return diff_x(stress[:, 0]) + diff_y(stress[:, 1, 1:-1]) + diff_z(stress[:, 2, 1:-1])

def advance_config(field, field_ext, spring_ext, flow, slopes, noise):
    grad_x, grad_y, grad_z = slopes
    along = flow[0] * diff_x(field_ext) + flow[1] * diff_y(field) + flow[2] * diff_z(field)
    stretch = grad_x * field[..., 0:1, :, :, :] + grad_y * field[..., 1:2, :, :, :] + grad_z * field[..., 2:3, :, :, :]
    spring = spring_ext[..., None, 1:-1, :, :]
    drift = -along + stretch - spring * field / (2.0 * relax_time)
    return field + time_step * drift + math.sqrt(time_step / relax_time) * noise

def velocity_rate(flow_ext, stress_div, y_start, count):
    padded = jnp.pad(flow_ext, ((0, 0), (0, 0), (1, 1), (0, 0)))
    window = lax.dynamic_slice_in_dim(padded, y_start, count + 2, 2)
    centre = window[:, 1:-1, 1:-1]
    grad_x = 0.5 * (window[:, 2:, 1:-1] - window[:, :-2, 1:-1])
    grad_y = 0.5 * (window[:, 1:-1, 2:] - window[:, 1:-1, :-2])
    grad_z = 0.5 * (jnp.roll(centre, -1, 3) - jnp.roll(centre, 1, 3))
    along = centre[0] * grad_x + centre[1] * grad_y + centre[2] * grad_z
    lap = window[:, 2:, 1:-1] + window[:, :-2, 1:-1] - 2.0 * centre
    lap = lap + (window[:, 1:-1, 2:] + window[:, 1:-1, :-2] - 2.0 * centre)
    lap = lap + (jnp.roll(centre, -1, 3) + jnp.roll(centre, 1, 3) - 2.0 * centre)
    return -along + viscosity * lap + stress_coef * stress_div

def reference(config_fields, velocity, noise_keys):
    fields, _, total_x, rows, depth = config_fields.shape
    cells = total_x * rows * depth
    index = cell_index(jnp.int32(0), total_x, total_x, rows, depth)
    config, flow = (config_fields, velocity)
    for step in range(STEPS):
        flow_ext = wrap_x(flow)
        slopes = (diff_x(flow_ext), diff_y(flow), diff_z(flow))

        def add_stress(total, field):
            field_ext = wrap_x(field)
            weighted = spring_factor(field_ext)[None] * field_ext
            return (total + weighted[:, None] * field_ext[None], None)
        empty = jnp.zeros((3, 3, total_x + 2, rows, depth), jnp.float32)
        stress, _ = lax.scan(add_stress, empty, config)
        stress_div = divergence(stress / fields)

        def advance(item):
            field, key = item
            field_ext = wrap_x(field)
            noise = gauss_noise(key, index)
            return advance_config(field, field_ext, spring_factor(field_ext), flow, slopes, noise)
        config = lax.map(advance, (config, noise_keys[:, step]))
        start = flow + time_step * velocity_rate(flow_ext, stress_div, jnp.int32(0), rows)
        flux = jnp.sum(start[0])
        flow = jnp.concatenate([start[:1] + (bulk_target - flux / cells), start[1:]], axis=0)
    return (config, flow)
```

```python
import functools
import math

import jax
import jax.numpy as jnp
from jax import lax
from jax.experimental import pallas as pl
from jax.experimental.pallas import tpu as pltpu
from jax.sharding import PartitionSpec as P

time_step = 0.05
viscosity = 0.5
stress_coef = 4.0
relax_time = 0.5
spring_limit = 10.0
spring_floor = 0.2
bulk_target = 1.0

SINE = (4.442882834149242, -7.308241154509167, 3.6062889576892747, -0.8457635932838079, 0.10920574854431932)
PAIRS = ((0, 0), (0, 1), (0, 2), (1, 1), (1, 2), (2, 2))
PLACE = ((0, 1, 2), (1, 3, 4), (2, 4, 5))
VMEM_LIMIT = 56 * 1024 * 1024
VMEM = pl.BlockSpec(memory_space=pltpu.VMEM)
SMEM = pl.BlockSpec(memory_space=pltpu.SMEM)


def params():
    return pltpu.CompilerParams(vmem_limit_bytes=VMEM_LIMIT)


def mix_bits(value):
    value = value ^ lax.shift_right_logical(value, jnp.int32(16))
    value = value * jnp.int32(73244475)
    value = value ^ lax.shift_right_logical(value, jnp.int32(16))
    value = value * jnp.int32(73244475)
    return value ^ lax.shift_right_logical(value, jnp.int32(16))


def noise_of(salted, even):
    mask = jnp.int32(16777215)
    first = mix_bits(even ^ salted)
    second = mix_bits(even ^ (salted ^ 1))
    upper = ((first & mask).astype(jnp.float32) + 0.5) * (1.0 / 16777216.0)
    turn = (second & mask).astype(jnp.float32) * (1.0 / 16777216.0) + (0.5 / 16777216.0 - 0.5)
    square = jnp.maximum(jnp.log(upper) * (-2.0 * time_step / relax_time), 1e-30)
    radius = square * lax.rsqrt(square)
    w = turn * turn
    q = jnp.float32(SINE[4])
    for coef in SINE[3::-1]:
        q = q * w + coef
    q = q * turn
    return radius * (q * q - 1.0)


def noise_kernel(step, total_x, keys_ref, out_ref):
    fields, _, width, rows, depth = out_ref.shape
    chunk = 32
    chunks = rows // chunk
    x_start = lax.axis_index("gx") * width
    salts = [mix_bits(keys_ref[k, step] + jnp.int32(40503)) for k in range(fields)]
    ypos = lax.broadcasted_iota(jnp.int32, (chunk, depth), 0)
    zpos = lax.broadcasted_iota(jnp.int32, (chunk, depth), 1)
    local = (ypos * depth + zpos) * 2

    def body(n, carry):
        comp = n // (width * chunks)
        rest = n - comp * (width * chunks)
        x = rest // chunks
        part = rest - x * chunks
        base = ((comp * total_x + x_start + x) * rows + part * chunk) * (2 * depth)
        even = local + base
        start = pl.multiple_of(part * chunk, chunk)
        for k in range(fields):
            out_ref[k, comp, x, pl.ds(start, chunk), :] = noise_of(salts[k], even)
        return carry

    lax.fori_loop(0, 3 * width * chunks, body, 0)


def draw_noise(keys, step, total_x, shape):
    return pl.pallas_call(
        functools.partial(noise_kernel, step, total_x),
        out_shape=jax.ShapeDtypeStruct(shape, jnp.float32),
        in_specs=[SMEM],
        out_specs=VMEM,
        compiler_params=params(),
        name="draw_noise",
    )(keys)


def up_z(f):
    return pltpu.roll(f, f.shape[-1] - 1, f.ndim - 1)


def down_z(f):
    return pltpu.roll(f, 1, f.ndim - 1)


def up_y(f):
    row = lax.broadcasted_iota(jnp.int32, f.shape, 0)
    return jnp.where(row == f.shape[0] - 1, 0.0, pltpu.roll(f, f.shape[0] - 1, 0))


def down_y(f):
    row = lax.broadcasted_iota(jnp.int32, f.shape, 0)
    return jnp.where(row == 0, 0.0, pltpu.roll(f, 1, 0))


def spring_of(q):
    length = q[0] * q[0] + q[1] * q[1] + q[2] * q[2]
    return 1.0 / jnp.maximum(1.0 - length * (1.0 / spring_limit), spring_floor)


def fill_stress(config_ref, stress_ref, total_fields):
    fields, _, width, rows, depth = config_ref.shape
    chunk = 32
    chunks = rows // chunk

    def body(n, carry):
        x = n // chunks
        start = pl.multiple_of((n - x * chunks) * chunk, chunk)
        totals = [None] * 6
        for k in range(fields):
            q = [config_ref[k, i, x, pl.ds(start, chunk), :] for i in range(3)]
            spring = spring_of(q) * (1.0 / total_fields)
            weighted = [spring * q[i] for i in range(3)]
            for p, (i, j) in enumerate(PAIRS):
                term = weighted[i] * q[j]
                totals[p] = term if k == 0 else totals[p] + term
        for p in range(6):
            stress_ref[p, x, pl.ds(start, chunk), :] = totals[p]
        return carry

    lax.fori_loop(0, width * chunks, body, 0)


def fill_divergence(stress_ref, div_ref, first_ref, last_ref):
    width = stress_ref.shape[1]
    for i in range(3):
        first_ref[i] = stress_ref[PLACE[i][0], 0]
        last_ref[i] = stress_ref[PLACE[i][0], width - 1]
        for x in range(width):
            sy = stress_ref[PLACE[i][1], x]
            sz = stress_ref[PLACE[i][2], x]
            total = up_y(sy) - down_y(sy) + up_z(sz) - down_z(sz)
            if x + 1 < width:
                total = total + stress_ref[PLACE[i][0], x + 1]
            if x > 0:
                total = total - stress_ref[PLACE[i][0], x - 1]
            div_ref[i, x] = 0.5 * total


def first_kernel(total_fields, config_ref, div_ref, first_ref, last_ref, stress_ref):
    fill_stress(config_ref, stress_ref, total_fields)
    fill_divergence(stress_ref, div_ref, first_ref, last_ref)


def first_stress(config, total_fields):
    _, _, width, rows, depth = config.shape
    end = jax.ShapeDtypeStruct((3, rows, depth), jnp.float32)
    return pl.pallas_call(
        functools.partial(first_kernel, total_fields),
        out_shape=[jax.ShapeDtypeStruct((3, width, rows, depth), jnp.float32), end, end],
        in_specs=[VMEM],
        out_specs=[VMEM] * 3,
        scratch_shapes=[pltpu.VMEM((6, width, rows, depth), jnp.float32)],
        compiler_params=params(),
        name="first_stress",
    )(config)


def advance_fields(config_ref, before_ref, after_ref, flow_ref, fbefore, fafter, noise_ref, new_ref, flow_at, slope_ref):
    fields, _, width, rows, depth = config_ref.shape
    half = 0.5 * time_step
    for x in range(width):
        for i in range(3):
            here = flow_at(i, x)
            below = flow_at(i, x - 1) if x > 0 else fbefore(i)
            above = flow_at(i, x + 1) if x + 1 < width else fafter(i)
            slope_ref[3 * i] = half * (above - below)
            slope_ref[3 * i + 1] = half * (up_y(here) - down_y(here))
            slope_ref[3 * i + 2] = half * (up_z(here) - down_z(here))
            slope_ref[9 + i] = half * here

        def body(k, carry, x=x):
            q = [config_ref[k, i, x] for i in range(3)]
            keep = 1.0 - (time_step / (2.0 * relax_time)) * spring_of(q)
            for i in range(3):
                below = config_ref[k, i, x - 1] if x > 0 else before_ref[k, i]
                above = config_ref[k, i, x + 1] if x + 1 < width else after_ref[k, i]
                along = slope_ref[9] * (above - below)
                along = along + slope_ref[10] * (up_y(q[i]) - down_y(q[i]))
                along = along + slope_ref[11] * (up_z(q[i]) - down_z(q[i]))
                stretch = slope_ref[3 * i] * q[0] + slope_ref[3 * i + 1] * q[1] + slope_ref[3 * i + 2] * q[2]
                new_ref[k, i, x] = q[i] * keep + (stretch - along) + noise_ref[k, i, x]
            return carry

        lax.fori_loop(0, fields, body, 0)


def second_kernel(
    total_fields, config_ref, before_ref, after_ref, flow_ref, fbefore_ref, fafter_ref, noise_ref,
    new_ref, div_ref, first_ref, last_ref, wall_ref, slope_ref, stress_ref,
):
    advance_fields(
        config_ref, before_ref, after_ref, flow_ref,
        lambda i: fbefore_ref[i], lambda i: fafter_ref[i], noise_ref, new_ref,
        lambda i, x: flow_ref[i, x], slope_ref,
    )
    fill_stress(new_ref, stress_ref, total_fields)
    fill_divergence(stress_ref, div_ref, first_ref, last_ref)
    width, rows, depth = stress_ref.shape[1:]
    wall = jnp.zeros((1, depth), jnp.float32)
    for x in range(width):
        wall = wall + (stress_ref[1, x, rows - 1:rows, :] - stress_ref[1, x, 0:1, :])
    wall_ref[...] = jnp.broadcast_to(0.5 * wall, (8, depth))


def second_fields(config, before, after, flow, fbefore, fafter, noise, total_fields):
    _, _, width, rows, depth = config.shape
    end = jax.ShapeDtypeStruct((3, rows, depth), jnp.float32)
    return pl.pallas_call(
        functools.partial(second_kernel, total_fields),
        out_shape=[
            jax.ShapeDtypeStruct(config.shape, jnp.float32),
            jax.ShapeDtypeStruct((3, width, rows, depth), jnp.float32),
            end,
            end,
            jax.ShapeDtypeStruct((8, depth), jnp.float32),
        ],
        in_specs=[VMEM] * 7,
        out_specs=[VMEM] * 5,
        scratch_shapes=[
            pltpu.VMEM((12, rows, depth), jnp.float32),
            pltpu.VMEM((6, width, rows, depth), jnp.float32),
        ],
        compiler_params=params(),
        name="second_fields",
    )(config, before, after, flow, fbefore, fafter, noise)


def flow_step(at, div_at, width, write):
    half = 0.5 * time_step
    for x in range(width):
        adv = [half * at(j, x) for j in range(3)]
        for i in range(3):
            here = at(i, x)
            below, above = at(i, x - 1), at(i, x + 1)
            left, right = down_y(here), up_y(here)
            back, front = down_z(here), up_z(here)
            along = adv[0] * (above - below) + adv[1] * (right - left) + adv[2] * (front - back)
            lap = (above + below) + (right + left) + (front + back) - 6.0 * here
            write(i, x, here - along + (time_step * viscosity) * lap + (time_step * stress_coef) * div_at(i, x))


def third_kernel(flow_ref, fbefore_ref, fafter_ref, div_ref, start_ref, first_ref, last_ref, sums_ref):
    _, width, rows, depth = flow_ref.shape

    def at(i, x):
        if x < 0:
            return fbefore_ref[i]
        if x >= width:
            return fafter_ref[i]
        return flow_ref[i, x]

    def write(i, x, value):
        start_ref[i, x] = value

    flow_step(at, lambda i, x: div_ref[i, x], width, write)
    total = jnp.zeros((8, depth), jnp.float32)
    bend = jnp.zeros((8, depth), jnp.float32)
    edge = jnp.zeros((1, depth), jnp.float32)
    gain = jnp.zeros((1, depth), jnp.float32)
    for x in range(width):
        s, v, w = start_ref[0, x], start_ref[1, x], start_ref[2, x]
        term = v * (0.5 * (up_y(s) - down_y(s))) + w * (0.5 * (up_z(s) - down_z(s)))
        for r in range(rows // 8):
            total = total + s[8 * r:8 * r + 8]
            bend = bend + term[8 * r:8 * r + 8]
        edge = edge + (s[0:1] + s[rows - 1:rows])
        gain = gain + (v[0:1] - v[rows - 1:rows])
    sums_ref[0:1] = jnp.sum(total, axis=0, keepdims=True)
    sums_ref[1:2] = jnp.sum(bend, axis=0, keepdims=True) + viscosity * edge
    sums_ref[2:3] = 0.5 * gain
    sums_ref[3:8] = jnp.zeros((5, depth), jnp.float32)
    for i in range(3):
        first_ref[i] = start_ref[i, 0]
        last_ref[i] = start_ref[i, width - 1]


def third_flow(flow, fbefore, fafter, div):
    _, width, rows, depth = flow.shape
    end = jax.ShapeDtypeStruct((3, rows, depth), jnp.float32)
    return pl.pallas_call(
        third_kernel,
        out_shape=[jax.ShapeDtypeStruct(flow.shape, jnp.float32), end, end, jax.ShapeDtypeStruct((8, depth), jnp.float32)],
        in_specs=[VMEM] * 4,
        out_specs=[VMEM] * 4,
        compiler_params=params(),
        name="third_flow",
    )(flow, fbefore, fafter, div)


def fourth_kernel(config_ref, before_ref, after_ref, start_ref, sbefore_ref, safter_ref, noise_ref, lift_ref, new_ref, slope_ref):
    lift = lift_ref[0]

    def flow_at(i, x):
        return start_ref[i, x] + lift if i == 0 else start_ref[i, x]

    advance_fields(
        config_ref, before_ref, after_ref, start_ref,
        lambda i: sbefore_ref[i] + lift if i == 0 else sbefore_ref[i],
        lambda i: safter_ref[i] + lift if i == 0 else safter_ref[i],
        noise_ref, new_ref, flow_at, slope_ref,
    )


def fourth_fields(config, before, after, start, sbefore, safter, noise, lift):
    rows, depth = config.shape[3:]
    return pl.pallas_call(
        fourth_kernel,
        out_shape=jax.ShapeDtypeStruct(config.shape, jnp.float32),
        in_specs=[VMEM] * 7 + [SMEM],
        out_specs=VMEM,
        scratch_shapes=[pltpu.VMEM((12, rows, depth), jnp.float32)],
        compiler_params=params(),
        name="fourth_fields",
    )(config, before, after, start, sbefore, safter, noise, lift)


def fifth_kernel(start_ref, sbefore_ref, safter_ref, div_ref, lift_ref, out_ref):
    width = start_ref.shape[1]
    lift = lift_ref[0]
    last_lift = lift_ref[1]

    def at(i, x):
        if x < 0:
            value = sbefore_ref[i]
        elif x >= width:
            value = safter_ref[i]
        else:
            value = start_ref[i, x]
        return value + lift if i == 0 else value

    def write(i, x, value):
        out_ref[i, x] = value + last_lift if i == 0 else value

    flow_step(at, lambda i, x: div_ref[i, x], width, write)


def fifth_flow(start, sbefore, safter, div, lift):
    return pl.pallas_call(
        fifth_kernel,
        out_shape=jax.ShapeDtypeStruct(start.shape, jnp.float32),
        in_specs=[VMEM] * 4 + [SMEM],
        out_specs=VMEM,
        compiler_params=params(),
        name="fifth_flow",
    )(start, sbefore, safter, div, lift)


def from_left(value):
    count = lax.axis_size("gx")
    return lax.ppermute(value, "gx", [(i, (i + 1) % count) for i in range(count)])


def from_right(value):
    count = lax.axis_size("gx")
    return lax.ppermute(value, "gx", [((i + 1) % count, i) for i in range(count)])


def row_sum(value):
    count = lax.axis_size("row")
    bit = 1
    while bit < count:
        value = value + lax.ppermute(value, "row", [(i, i ^ bit) for i in range(count)])
        bit *= 2
    return value


def with_ends(div, before, after):
    first = div[:, :1] - 0.5 * before[:, None]
    last = div[:, -1:] + 0.5 * after[:, None]
    return jnp.concatenate([first, div[:, 1:-1], last], axis=1)


def shards(config, flow, keys):
    fields, _, width, rows, depth = config.shape
    total_fields = fields * lax.axis_size("row")
    slabs = lax.axis_size("gx")
    total_x = width * slabs
    cells = total_x * rows * depth

    div, first, last = first_stress(config, total_fields)
    ends = from_left(last), from_right(first)
    head = jnp.concatenate([config[:, :, 0], flow[None, :, 0]], axis=0)
    tail = jnp.concatenate([config[:, :, -1], flow[None, :, -1]], axis=0)
    left, right = from_left(tail), from_right(head)
    noise = draw_noise(keys, 0, total_x, config.shape)
    later = draw_noise(keys, 1, total_x, config.shape)
    div = row_sum(with_ends(div, *ends))

    fleft, fright = left[fields], right[fields]
    config, next_div, first, last, wall = second_fields(
        config, left[:fields], right[:fields], flow, fleft, fright, noise, total_fields
    )
    ends = from_left(last), from_right(first)
    left, right = from_left(config[:, :, -1]), from_right(config[:, :, 0])
    next_div = row_sum(with_ends(next_div, *ends))
    wall = row_sum(wall)

    start, first, last, sums = third_flow(flow, fleft, fright, div)
    sleft, sright = from_left(last), from_right(first)
    mine = jnp.concatenate([sums[:3], wall[:1], sums[3:7]], axis=0)
    shared = lax.all_to_all(jnp.broadcast_to(mine[None], (slabs, 8, depth)), "gx", 0, 0)
    sums = jnp.sum(shared, axis=(0, 2))
    lift = bulk_target - sums[0] / cells
    change = time_step * (stress_coef * sums[3] - sums[1] - lift * (sums[2] + 2.0 * viscosity * total_x * depth))
    lifts = jnp.stack([lift, -change / cells])

    config = fourth_fields(config, left, right, start, sleft, sright, later, lifts)
    flow = fifth_flow(start, sleft, sright, next_div, lifts)
    return config, flow


def solution(mesh):
    placed = (P("row", None, "gx", None, None), P(None, "gx", None, None), P("row", None))
    return jax.shard_map(
        shards,
        mesh=mesh,
        in_specs=placed,
        out_specs=(P("row", None, "gx", None, None), P(None, "gx", None, None)),
        check_vma=False,
    )
```

```python
import functools
import math

import jax
import jax.numpy as jnp
from jax import lax
from jax.experimental import pallas as pl
from jax.experimental.pallas import tpu as pltpu
from jax.sharding import PartitionSpec as P

time_step = 0.05
viscosity = 0.5
stress_coef = 4.0
relax_time = 0.5
spring_limit = 10.0
spring_floor = 0.2
bulk_target = 1.0

SINE = (4.442882834149242, -7.308241154509167, 3.6062889576892747, -0.8457635932838079, 0.10920574854431932)
PAIRS = ((0, 0), (0, 1), (0, 2), (1, 1), (1, 2), (2, 2))
PLACE = ((0, 1, 2), (1, 3, 4), (2, 4, 5))
VMEM_LIMIT = 20 * 1024 * 1024
SMEM = pl.BlockSpec(memory_space=pltpu.SMEM)


def params():
    return pltpu.CompilerParams(vmem_limit_bytes=VMEM_LIMIT)


def mix_bits(value):
    value = value ^ lax.shift_right_logical(value, jnp.int32(16))
    value = value * jnp.int32(73244475)
    value = value ^ lax.shift_right_logical(value, jnp.int32(16))
    value = value * jnp.int32(73244475)
    return value ^ lax.shift_right_logical(value, jnp.int32(16))


def noise_of(salted, even):
    mask = jnp.int32(16777215)
    first = mix_bits(even ^ salted)
    second = mix_bits(even ^ (salted ^ 1))
    upper = ((first & mask).astype(jnp.float32) + 0.5) * (1.0 / 16777216.0)
    turn = (second & mask).astype(jnp.float32) * (1.0 / 16777216.0) + (0.5 / 16777216.0 - 0.5)
    square = jnp.maximum(jnp.log(upper) * (-2.0 * time_step / relax_time), 1e-30)
    radius = square * lax.rsqrt(square)
    w = turn * turn
    q = jnp.float32(SINE[4])
    for coef in SINE[3::-1]:
        q = q * w + coef
    q = q * turn
    return radius * (q * q - 1.0)


def noise_kernel(step, total_x, keys_ref, out_ref):
    _, _, width, rows, depth = out_ref.shape
    x_start = lax.axis_index("gx") * width
    salted = mix_bits(keys_ref[2 * pl.program_id(0) + step] + jnp.int32(40503))
    ypos = lax.broadcasted_iota(jnp.int32, (rows, depth), 0)
    zpos = lax.broadcasted_iota(jnp.int32, (rows, depth), 1)
    local = (ypos * depth + zpos) * 2

    def body(n, carry):
        comp = n // width
        x = n - comp * width
        even = local + ((comp * total_x + x_start + x) * rows) * (2 * depth)
        out_ref[0, comp, x] = noise_of(salted, even)
        return carry

    lax.fori_loop(0, 3 * width, body, 0)


def draw_noise(keys, step, total_x, shape):
    fields, comps, width, rows, depth = shape
    return pl.pallas_call(
        functools.partial(noise_kernel, step, total_x),
        grid=(fields,),
        out_shape=pltpu.HBM(shape, jnp.float32) if step else jax.ShapeDtypeStruct(shape, jnp.float32),
        in_specs=[SMEM],
        out_specs=pl.BlockSpec((1, comps, width, rows, depth), lambda k: (k, 0, 0, 0, 0)),
        compiler_params=params(),
        name="draw_noise",
    )(keys)


def up_z(f):
    return pltpu.roll(f, f.shape[-1] - 1, f.ndim - 1)


def down_z(f):
    return pltpu.roll(f, 1, f.ndim - 1)


def up_y(f):
    row = lax.broadcasted_iota(jnp.int32, f.shape, 0)
    return jnp.where(row == f.shape[0] - 1, 0.0, pltpu.roll(f, f.shape[0] - 1, 0))


def down_y(f):
    row = lax.broadcasted_iota(jnp.int32, f.shape, 0)
    return jnp.where(row == 0, 0.0, pltpu.roll(f, 1, 0))


def spring_of(q):
    length = q[0] * q[0] + q[1] * q[1] + q[2] * q[2]
    return 1.0 / jnp.maximum(1.0 - length * (1.0 / spring_limit), spring_floor)


def field_block(shape):
    return pl.BlockSpec((1,) + shape[1:], lambda k: (k,) + (0,) * (len(shape) - 1))


def whole_block(shape):
    return pl.BlockSpec(shape, lambda k: (0,) * len(shape))


def rim_block(shape, at=None):
    if at is None:
        return pl.BlockSpec((1,) + shape[1:], lambda k: (k, 0, 0, 0))
    return pl.BlockSpec((1,) + shape[1:], lambda k: (at, 0, 0, 0))


def quad_place():
    return lax.rem(lax.axis_index("row"), 4)


def div_kernel(total_fields, config_ref, before_ref, after_ref, *refs):
    outs, stress_ref, rim_ref, div_ref = refs[:4], refs[4], refs[5], refs[6]
    k = pl.program_id(0)
    _, _, width, rows, depth = config_ref.shape

    @pl.when(k == 0)
    def _():
        stress_ref[...] = jnp.zeros_like(stress_ref)
        rim_ref[...] = jnp.zeros_like(rim_ref)

    for x in range(width):
        q = [config_ref[0, i, x] for i in range(3)]
        spring = spring_of(q) * (0.5 / total_fields)
        weighted = [spring * q[i] for i in range(3)]
        for p, (i, j) in enumerate(PAIRS):
            stress_ref[p, x] += weighted[i] * q[j]
    for side, ref in enumerate((before_ref, after_ref)):
        q = [ref[0, i] for i in range(3)]
        weighted = spring_of(q) * (0.5 / total_fields) * q[0]
        for i in range(3):
            rim_ref[side, i] += weighted * q[i]

    @pl.when(k == pl.num_programs(0) - 1)
    def _():
        for x in range(width):
            for i in range(3):
                sy = stress_ref[PLACE[i][1], x]
                sz = stress_ref[PLACE[i][2], x]
                above = stress_ref[PLACE[i][0], x + 1] if x + 1 < width else rim_ref[1, i]
                below = stress_ref[PLACE[i][0], x - 1] if x > 0 else rim_ref[0, i]
                div_ref[x, i] = (above - below) + (up_y(sy) - down_y(sy)) + (up_z(sz) - down_z(sz))
        place = quad_place()
        for n, out in enumerate(outs):
            out[...] = div_ref[lax.rem(place + n, 4)]


def stress_parts(config, before, after, total_fields):
    fields, _, width, rows, depth = config.shape
    part = jax.ShapeDtypeStruct((3, rows, depth), jnp.float32)
    return pl.pallas_call(
        functools.partial(div_kernel, total_fields),
        grid=(fields,),
        out_shape=[part] * 4,
        in_specs=[field_block(config.shape), rim_block(before.shape), rim_block(after.shape)],
        out_specs=[whole_block(part.shape)] * 4,
        scratch_shapes=[
            pltpu.VMEM((6, width, rows, depth), jnp.float32),
            pltpu.VMEM((2, 3, rows, depth), jnp.float32),
            pltpu.VMEM((width, 3, rows, depth), jnp.float32),
        ],
        compiler_params=params(),
        name="stress_parts",
    )(config, before, after)


def fill_slopes(flow_at, slope_ref, width):
    half = 0.5 * time_step
    for x in range(width):
        for i in range(3):
            here = flow_at(i, x)
            slope_ref[x, 3 * i] = half * (flow_at(i, x + 1) - flow_at(i, x - 1))
            slope_ref[x, 3 * i + 1] = half * (up_y(here) - down_y(here))
            slope_ref[x, 3 * i + 2] = half * (up_z(here) - down_z(here))
            slope_ref[x, 9 + i] = half * here


def advance_field(config_ref, before_ref, after_ref, noise_ref, new_ref, slope_ref):
    _, _, width, rows, depth = config_ref.shape
    for x in range(width):
        q = [config_ref[0, i, x] for i in range(3)]
        keep = 1.0 - (time_step / (2.0 * relax_time)) * spring_of(q)
        for i in range(3):
            below = config_ref[0, i, x - 1] if x > 0 else before_ref[0, i]
            above = config_ref[0, i, x + 1] if x + 1 < width else after_ref[0, i]
            along = slope_ref[x, 9] * (above - below)
            along = along + slope_ref[x, 10] * (up_y(q[i]) - down_y(q[i]))
            along = along + slope_ref[x, 11] * (up_z(q[i]) - down_z(q[i]))
            stretch = slope_ref[x, 3 * i] * q[0] + slope_ref[x, 3 * i + 1] * q[1] + slope_ref[x, 3 * i + 2] * q[2]
            new_ref[0, i, x] = q[i] * keep + (stretch - along) + noise_ref[0, i, x]


def second_kernel(
    total_fields, config_ref, before_ref, after_ref, flow_ref, fbefore_ref, fafter_ref, noise_ref,
    new_ref, first_ref, last_ref, wall_ref, slope_ref,
):
    k = pl.program_id(0)
    _, _, width, rows, depth = config_ref.shape

    def flow_at(i, x):
        if x < 0:
            return fbefore_ref[0, i]
        if x >= width:
            return fafter_ref[0, i]
        return flow_ref[i, x]

    @pl.when(k == 0)
    def _():
        fill_slopes(flow_at, slope_ref, width)
        wall_ref[...] = jnp.zeros_like(wall_ref)

    advance_field(config_ref, before_ref, after_ref, noise_ref, new_ref, slope_ref)
    for i in range(3):
        first_ref[0, i] = new_ref[0, i, 0]
        last_ref[0, i] = new_ref[0, i, width - 1]
    wall = jnp.zeros((8, depth), jnp.float32)
    row = lax.broadcasted_iota(jnp.int32, (8, depth), 0)
    for x in range(width):
        low = [new_ref[0, i, x, 0:8, :] for i in range(3)]
        high = [new_ref[0, i, x, rows - 8:rows, :] for i in range(3)]
        wall = wall + jnp.where(row == 7, spring_of(high) * (high[0] * high[1]), 0.0)
        wall = wall - jnp.where(row == 0, spring_of(low) * (low[0] * low[1]), 0.0)
    wall_ref[...] += wall * (0.5 / total_fields)


def second_fields(config, before, after, flow, noise, total_fields):
    fields, _, width, rows, depth = config.shape
    rim = jax.ShapeDtypeStruct((fields, 3, rows, depth), jnp.float32)
    wall = jax.ShapeDtypeStruct((8, depth), jnp.float32)
    return pl.pallas_call(
        functools.partial(second_kernel, total_fields),
        grid=(fields,),
        out_shape=[pltpu.HBM(config.shape, jnp.float32), rim, rim, wall],
        in_specs=[
            field_block(config.shape), rim_block(before.shape), rim_block(after.shape), whole_block(flow.shape),
            rim_block(before.shape, fields), rim_block(after.shape, fields), field_block(noise.shape),
        ],
        out_specs=[field_block(config.shape), rim_block(rim.shape), rim_block(rim.shape), whole_block(wall.shape)],
        scratch_shapes=[pltpu.VMEM((width, 12, rows, depth), jnp.float32)],
        compiler_params=params(),
        name="second_fields",
    )(config, before, after, flow, before, after, noise)


def flow_step(at, div_at, width, write):
    half = 0.5 * time_step
    for x in range(width):
        adv = [half * at(j, x) for j in range(3)]
        for i in range(3):
            here = at(i, x)
            below, above = at(i, x - 1), at(i, x + 1)
            left, right = down_y(here), up_y(here)
            back, front = down_z(here), up_z(here)
            along = adv[0] * (above - below) + adv[1] * (right - left) + adv[2] * (front - back)
            lap = (above + below) + (right + left) + (front + back) - 6.0 * here
            write(i, x, here - along + (time_step * viscosity) * lap + (time_step * stress_coef) * div_at(i, x))


def gather_parts(parts, div_ref):
    place = quad_place()
    for n, part in enumerate(parts):
        at = lax.rem(place + 4 - n, 4)
        rows = div_ref.shape[2]
        for i in range(3):
            div_ref[at, i] = part[i * rows:(i + 1) * rows]


def third_kernel(flow_ref, fbefore_ref, fafter_ref, p0, p1, p2, p3, start_ref, first_ref, last_ref, sums_ref, div_ref):
    _, width, rows, depth = flow_ref.shape
    gather_parts((p0, p1, p2, p3), div_ref)

    def at(i, x):
        if x < 0:
            return fbefore_ref[0, i]
        if x >= width:
            return fafter_ref[0, i]
        return flow_ref[i, x]

    def write(i, x, value):
        start_ref[i, x] = value

    flow_step(at, lambda i, x: div_ref[x, i], width, write)
    total = jnp.zeros((8, depth), jnp.float32)
    bend = jnp.zeros((8, depth), jnp.float32)
    edge = jnp.zeros((1, depth), jnp.float32)
    gain = jnp.zeros((1, depth), jnp.float32)
    for x in range(width):
        s, v, w = start_ref[0, x], start_ref[1, x], start_ref[2, x]
        term = v * (0.5 * (up_y(s) - down_y(s))) + w * (0.5 * (up_z(s) - down_z(s)))
        for r in range(rows // 8):
            total = total + s[8 * r:8 * r + 8]
            bend = bend + term[8 * r:8 * r + 8]
        edge = edge + (s[0:1] + s[rows - 1:rows])
        gain = gain + (v[0:1] - v[rows - 1:rows])
    row = lax.broadcasted_iota(jnp.int32, (8, depth), 0)
    sums = [
        jnp.sum(total, axis=0, keepdims=True),
        jnp.sum(bend, axis=0, keepdims=True) + viscosity * edge,
        0.5 * gain,
        jnp.sum(sum(p[3 * rows:] for p in (p0, p1, p2, p3)), axis=0, keepdims=True),
    ]
    tile = jnp.zeros((8, depth), jnp.float32)
    for n, value in enumerate(sums):
        tile = jnp.where(row == n, value, tile)
    for n in range(sums_ref.shape[0]):
        sums_ref[n] = tile
    for i in range(3):
        first_ref[i] = start_ref[i, 0]
        last_ref[i] = start_ref[i, width - 1]


def third_flow(flow, left, right, parts, slabs):
    _, width, rows, depth = flow.shape
    end = jax.ShapeDtypeStruct((3, rows, depth), jnp.float32)
    sums = jax.ShapeDtypeStruct((slabs, 8, depth), jnp.float32)
    at = left.shape[0] - 1
    return pl.pallas_call(
        third_kernel,
        grid=(1,),
        out_shape=[pltpu.HBM(flow.shape, jnp.float32), end, end, sums],
        in_specs=[whole_block(flow.shape), rim_block(left.shape, at), rim_block(right.shape, at)]
        + [whole_block(parts[0].shape)] * 4,
        out_specs=[whole_block(flow.shape), whole_block(end.shape), whole_block(end.shape), whole_block(sums.shape)],
        scratch_shapes=[pltpu.VMEM((width, 3, rows, depth), jnp.float32)],
        compiler_params=params(),
        name="third_flow",
    )(flow, left, right, *parts)


def lifts_of(shared_ref, walls, cells):
    sums = jnp.sum(jnp.sum(shared_ref[...], axis=0), axis=1, keepdims=True)
    lift = bulk_target - sums[0:1] / cells
    change = time_step * (stress_coef * sums[3:4] - sums[1:2] - lift * (sums[2:3] + 2.0 * viscosity * walls))
    return lift, -change / cells


def fourth_kernel(walls, cells, config_ref, before_ref, after_ref, start_ref, sbefore_ref, safter_ref, noise_ref, shared_ref, new_ref, slope_ref):
    width = config_ref.shape[2]

    def flow_at(i, x):
        if x < 0:
            return sbefore_ref[i]
        if x >= width:
            return safter_ref[i]
        return start_ref[i, x]

    @pl.when(pl.program_id(0) == 0)
    def _():
        lift = lifts_of(shared_ref, walls, cells)[0]
        fill_slopes(lambda i, x: flow_at(i, x) + lift if i == 0 else flow_at(i, x), slope_ref, width)

    advance_field(config_ref, before_ref, after_ref, noise_ref, new_ref, slope_ref)


def fourth_fields(config, before, after, start, sbefore, safter, noise, shared, walls, cells):
    fields, _, width, rows, depth = config.shape
    return pl.pallas_call(
        functools.partial(fourth_kernel, walls, cells),
        grid=(fields,),
        out_shape=jax.ShapeDtypeStruct(config.shape, jnp.float32),
        in_specs=[
            field_block(config.shape), rim_block(before.shape), rim_block(after.shape), whole_block(start.shape),
            whole_block(sbefore.shape), whole_block(safter.shape), field_block(noise.shape), whole_block(shared.shape),
        ],
        out_specs=field_block(config.shape),
        scratch_shapes=[pltpu.VMEM((width, 12, rows, depth), jnp.float32)],
        compiler_params=params(),
        name="fourth_fields",
    )(config, before, after, start, sbefore, safter, noise, shared)


def fifth_kernel(walls, cells, start_ref, sbefore_ref, safter_ref, p0, p1, p2, p3, shared_ref, out_ref, div_ref):
    width = start_ref.shape[1]
    lift, last_lift = lifts_of(shared_ref, walls, cells)
    gather_parts((p0, p1, p2, p3), div_ref)

    def at(i, x):
        if x < 0:
            value = sbefore_ref[i]
        elif x >= width:
            value = safter_ref[i]
        else:
            value = start_ref[i, x]
        return value + lift if i == 0 else value

    def write(i, x, value):
        out_ref[i, x] = value + last_lift if i == 0 else value

    flow_step(at, lambda i, x: div_ref[x, i], width, write)


def fifth_flow(start, sbefore, safter, parts, shared, walls, cells):
    _, width, rows, depth = start.shape
    return pl.pallas_call(
        functools.partial(fifth_kernel, walls, cells),
        grid=(1,),
        out_shape=jax.ShapeDtypeStruct(start.shape, jnp.float32),
        in_specs=[whole_block(start.shape)] + [whole_block(sbefore.shape)] * 2 + [whole_block(parts[0].shape)] * 4 + [whole_block(shared.shape)],
        out_specs=whole_block(start.shape),
        scratch_shapes=[pltpu.VMEM((width, 3, rows, depth), jnp.float32)],
        compiler_params=params(),
        name="fifth_flow",
    )(start, sbefore, safter, *parts, shared)


def pack_kernel(first_ref, last_ref, ffirst_ref, flast_ref, head_ref, tail_ref):
    velocity = pl.program_id(0) == pl.num_programs(0) - 1

    @pl.when(velocity)
    def _():
        head_ref[0] = ffirst_ref[:, 0]
        tail_ref[0] = flast_ref[:, 0]

    @pl.when(jnp.logical_not(velocity))
    def _():
        head_ref[0] = first_ref[0, :, 0]
        tail_ref[0] = last_ref[0, :, 0]


def pack_ends(config, flow):
    fields, _, width, rows, depth = config.shape
    rim = jax.ShapeDtypeStruct((fields + 1, 3, rows, depth), jnp.float32)

    def layer(x):
        return pl.BlockSpec((1, 3, 1, rows, depth), lambda k: (jnp.minimum(k, fields - 1), 0, x, 0, 0))

    def flow_layer(x):
        return pl.BlockSpec((3, 1, rows, depth), lambda k: (0, x, 0, 0))

    return pl.pallas_call(
        pack_kernel,
        grid=(fields + 1,),
        out_shape=[rim, rim],
        in_specs=[layer(0), layer(width - 1), flow_layer(0), flow_layer(width - 1)],
        out_specs=[rim_block(rim.shape)] * 2,
        compiler_params=params(),
        name="pack_ends",
    )(config, config, flow, flow)


def from_left(value):
    count = lax.axis_size("gx")
    return lax.ppermute(value, "gx", [(i, (i + 1) % count) for i in range(count)])


def from_right(value):
    count = lax.axis_size("gx")
    return lax.ppermute(value, "gx", [((i + 1) % count, i) for i in range(count)])


def quad_shift(value, by):
    count = lax.axis_size("row")
    return lax.ppermute(value, "row", [(i, i - i % 4 + (i + by) % 4) for i in range(count)])


def pair_swap(value, bit):
    count = lax.axis_size("row")
    return lax.ppermute(value, "row", [(i, i ^ bit) for i in range(count)])


def in_hbm(value):
    return pltpu.with_memory_space_constraint(value, pltpu.HBM)


def flat(value):
    return value.reshape(-1, value.shape[-1])


def after(value, *others):
    return lax.optimization_barrier((value,) + others)[0]


def shards(config, flow, keys):
    fields, _, width, rows, depth = config.shape
    total_fields = fields * lax.axis_size("row")
    slabs = lax.axis_size("gx")
    total_x = width * slabs
    cells = total_x * rows * depth

    keys = keys.reshape(-1)

    head, tail = pack_ends(in_hbm(config), in_hbm(flow))
    left, right = from_left(tail), from_right(head)
    noise = draw_noise(keys, 0, total_x, config.shape)
    left, right = after(left, noise), after(right, noise)

    parts = stress_parts(config, left, right, total_fields)
    got = [quad_shift(parts[n], n) for n in (1, 2, 3)]
    config, first, last, wall = second_fields(config, after(left, parts[0]), right, flow, noise, total_fields)
    before, behind = from_left(last), from_right(first)
    got = [after(g, config) for g in got]
    own = jnp.concatenate([flat(parts[0] + got[0] + got[1] + got[2]), wall], axis=0)
    swap = pair_swap(own, 4)
    later = draw_noise(after(keys, own), 1, total_x, config.shape)
    own = own + after(swap, later)
    div = [own] + [quad_shift(own, n) for n in (1, 2, 3)]

    parts = stress_parts(after(config, own), before, behind, total_fields)
    got = [quad_shift(parts[n], n) for n in (1, 2, 3)]

    start, first, last, sums = third_flow(flow, left, right, [after(d, parts[0]) for d in div], slabs)
    sleft, sright = from_left(last), from_right(first)
    shared = lax.all_to_all(sums, "gx", 0, 0)
    own = flat(parts[0] + got[0] + got[1] + after(got[2], start))
    own = own + after(pair_swap(own, 4), shared)
    next_div = [own] + [quad_shift(own, n) for n in (1, 2, 3)]

    walls = total_x * depth
    config = fourth_fields(in_hbm(config), in_hbm(before), in_hbm(behind), in_hbm(start), sleft, sright, in_hbm(later), shared, walls, cells)
    flow = fifth_flow(in_hbm(start), sleft, sright, [after(d, config) for d in next_div], shared, walls, cells)
    return config, flow


def solution(mesh):
    placed = (P("row", None, "gx", None, None), P(None, "gx", None, None), P("row", None))
    return jax.shard_map(
        shards,
        mesh=mesh,
        in_specs=placed,
        out_specs=(P("row", None, "gx", None, None), P(None, "gx", None, None)),
        check_vma=False,
    )
```

```python
import functools
import math

import jax
import jax.numpy as jnp
from jax import lax
from jax.experimental import pallas as pl
from jax.experimental.pallas import tpu as pltpu
from jax.sharding import PartitionSpec as P

time_step = 0.05
viscosity = 0.5
stress_coef = 4.0
relax_time = 0.5
spring_limit = 10.0
spring_floor = 0.2
bulk_target = 1.0

SINE = (4.442882834149242, -7.308241154509167, 3.6062889576892747, -0.8457635932838079, 0.10920574854431932)
PAIRS = ((0, 0), (0, 1), (0, 2), (1, 1), (1, 2), (2, 2))
PLACE = ((0, 1, 2), (1, 3, 4), (2, 4, 5))
VMEM_LIMIT = 20 * 1024 * 1024
SMEM = pl.BlockSpec(memory_space=pltpu.SMEM)


def params():
    return pltpu.CompilerParams(vmem_limit_bytes=VMEM_LIMIT)


def mix_bits(value):
    value = value ^ lax.shift_right_logical(value, jnp.int32(16))
    value = value * jnp.int32(73244475)
    value = value ^ lax.shift_right_logical(value, jnp.int32(16))
    value = value * jnp.int32(73244475)
    return value ^ lax.shift_right_logical(value, jnp.int32(16))


def noise_of(salted, even):
    mask = jnp.int32(16777215)
    first = mix_bits(even ^ salted)
    second = mix_bits(even ^ (salted ^ 1))
    upper = ((first & mask).astype(jnp.float32) + 0.5) * (1.0 / 16777216.0)
    turn = (second & mask).astype(jnp.float32) * (1.0 / 16777216.0) + (0.5 / 16777216.0 - 0.5)
    square = jnp.maximum(jnp.log(upper) * (-2.0 * time_step / relax_time), 1e-30)
    radius = square * lax.rsqrt(square)
    w = turn * turn
    q = jnp.float32(SINE[4])
    for coef in SINE[3::-1]:
        q = q * w + coef
    q = q * turn
    return radius * (q * q - 1.0)


def noise_kernel(step, total_x, keys_ref, out_ref):
    _, _, width, rows, depth = out_ref.shape
    x_start = lax.axis_index("gx") * width
    salted = mix_bits(keys_ref[2 * pl.program_id(0) + step] + jnp.int32(40503))
    ypos = lax.broadcasted_iota(jnp.int32, (rows, depth), 0)
    zpos = lax.broadcasted_iota(jnp.int32, (rows, depth), 1)
    local = (ypos * depth + zpos) * 2

    def body(n, carry):
        comp = n // width
        x = n - comp * width
        even = local + ((comp * total_x + x_start + x) * rows) * (2 * depth)
        out_ref[0, comp, x] = noise_of(salted, even)
        return carry

    lax.fori_loop(0, 3 * width, body, 0)


def draw_noise(keys, step, total_x, shape):
    fields, comps, width, rows, depth = shape
    return pl.pallas_call(
        functools.partial(noise_kernel, step, total_x),
        grid=(fields,),
        out_shape=pltpu.HBM(shape, jnp.float32) if step else jax.ShapeDtypeStruct(shape, jnp.float32),
        in_specs=[SMEM],
        out_specs=pl.BlockSpec((1, comps, width, rows, depth), lambda k: (k, 0, 0, 0, 0)),
        compiler_params=params(),
        name="draw_noise",
    )(keys)


def up_z(f):
    return pltpu.roll(f, f.shape[-1] - 1, f.ndim - 1)


def down_z(f):
    return pltpu.roll(f, 1, f.ndim - 1)


def up_y(f):
    row = lax.broadcasted_iota(jnp.int32, f.shape, 0)
    return jnp.where(row == f.shape[0] - 1, 0.0, pltpu.roll(f, f.shape[0] - 1, 0))


def down_y(f):
    row = lax.broadcasted_iota(jnp.int32, f.shape, 0)
    return jnp.where(row == 0, 0.0, pltpu.roll(f, 1, 0))


def spring_of(q):
    length = q[0] * q[0] + q[1] * q[1] + q[2] * q[2]
    return 1.0 / jnp.maximum(1.0 - length * (1.0 / spring_limit), spring_floor)


def field_block(shape):
    return pl.BlockSpec((1,) + shape[1:], lambda k: (k,) + (0,) * (len(shape) - 1))


def whole_block(shape):
    return pl.BlockSpec(shape, lambda k: (0,) * len(shape))


def rim_block(shape, at=None):
    if at is None:
        return pl.BlockSpec((1,) + shape[1:], lambda k: (k, 0, 0, 0))
    return pl.BlockSpec((1,) + shape[1:], lambda k: (at, 0, 0, 0))


def quad_place():
    return lax.rem(lax.axis_index("row"), 4)


def inner_kernel(total_fields, config_ref, stress_ref):
    k = pl.program_id(0)

    def add(first):
        for x in range(config_ref.shape[2]):
            q = [config_ref[0, i, x] for i in range(3)]
            spring = spring_of(q) * (0.5 / total_fields)
            weighted = [spring * q[i] for i in range(3)]
            for p, (i, j) in enumerate(PAIRS):
                term = weighted[i] * q[j]
                stress_ref[p, x] = term if first else stress_ref[p, x] + term

    @pl.when(k == 0)
    def _():
        add(True)

    @pl.when(k > 0)
    def _():
        add(False)


def inner_stress(config, total_fields):
    fields, _, width, rows, depth = config.shape
    stress = jax.ShapeDtypeStruct((6, width, rows, depth), jnp.float32)
    return pl.pallas_call(
        functools.partial(inner_kernel, total_fields),
        grid=(fields,),
        out_shape=stress,
        in_specs=[field_block(config.shape)],
        out_specs=whole_block(stress.shape),
        compiler_params=params(),
        name="inner_stress",
    )(config)


def parts_kernel(total_fields, fields, stress_ref, before_ref, after_ref, *refs):
    outs, rim_ref = refs[:4], refs[4]
    width = stress_ref.shape[1]
    for side, ref in enumerate((before_ref, after_ref)):
        totals = None
        for k in range(fields):
            q = [ref[k, i] for i in range(3)]
            weighted = spring_of(q) * (0.5 / total_fields) * q[0]
            terms = [weighted * q[i] for i in range(3)]
            totals = terms if k == 0 else [t + u for t, u in zip(totals, terms)]
        for i in range(3):
            rim_ref[(width + 1) * side, i] = totals[i]
    for x in range(width):
        for i in range(3):
            rim_ref[x + 1, i] = stress_ref[PLACE[i][0], x]
    place = quad_place()
    for n, out in enumerate(outs):
        x = lax.rem(place + n, 4)
        for i in range(3):
            sy = stress_ref[PLACE[i][1], x]
            sz = stress_ref[PLACE[i][2], x]
            out[i] = (rim_ref[x + 2, i] - rim_ref[x, i]) + (up_y(sy) - down_y(sy)) + (up_z(sz) - down_z(sz))


def stress_parts(stress, before, after, fields, total_fields):
    _, width, rows, depth = stress.shape
    part = jax.ShapeDtypeStruct((3, rows, depth), jnp.float32)
    rim = (fields,) + before.shape[1:]
    return pl.pallas_call(
        functools.partial(parts_kernel, total_fields, fields),
        grid=(1,),
        out_shape=[part] * 4,
        in_specs=[whole_block(stress.shape), whole_block(rim), whole_block(rim)],
        out_specs=[whole_block(part.shape)] * 4,
        scratch_shapes=[pltpu.VMEM((width + 2, 3, rows, depth), jnp.float32)],
        compiler_params=params(),
        name="stress_parts",
    )(stress, before, after)


def fill_slopes(flow_at, slope_ref, width):
    half = 0.5 * time_step
    for x in range(width):
        for i in range(3):
            here = flow_at(i, x)
            slope_ref[x, 3 * i] = half * (flow_at(i, x + 1) - flow_at(i, x - 1))
            slope_ref[x, 3 * i + 1] = half * (up_y(here) - down_y(here))
            slope_ref[x, 3 * i + 2] = half * (up_z(here) - down_z(here))
            slope_ref[x, 9 + i] = half * here


def advance_field(config_ref, before_ref, after_ref, noise_ref, new_ref, slope_ref):
    _, _, width, rows, depth = config_ref.shape
    for x in range(width):
        q = [config_ref[0, i, x] for i in range(3)]
        keep = 1.0 - (time_step / (2.0 * relax_time)) * spring_of(q)
        for i in range(3):
            below = config_ref[0, i, x - 1] if x > 0 else before_ref[0, i]
            above = config_ref[0, i, x + 1] if x + 1 < width else after_ref[0, i]
            along = slope_ref[x, 9] * (above - below)
            along = along + slope_ref[x, 10] * (up_y(q[i]) - down_y(q[i]))
            along = along + slope_ref[x, 11] * (up_z(q[i]) - down_z(q[i]))
            stretch = slope_ref[x, 3 * i] * q[0] + slope_ref[x, 3 * i + 1] * q[1] + slope_ref[x, 3 * i + 2] * q[2]
            new_ref[0, i, x] = q[i] * keep + (stretch - along) + noise_ref[0, i, x]


def second_kernel(
    total_fields, config_ref, before_ref, after_ref, flow_ref, fbefore_ref, fafter_ref, noise_ref,
    new_ref, first_ref, last_ref, wall_ref, slope_ref,
):
    k = pl.program_id(0)
    _, _, width, rows, depth = config_ref.shape

    def flow_at(i, x):
        if x < 0:
            return fbefore_ref[0, i]
        if x >= width:
            return fafter_ref[0, i]
        return flow_ref[i, x]

    @pl.when(k == 0)
    def _():
        fill_slopes(flow_at, slope_ref, width)
        wall_ref[...] = jnp.zeros_like(wall_ref)

    advance_field(config_ref, before_ref, after_ref, noise_ref, new_ref, slope_ref)
    for i in range(3):
        first_ref[0, i] = new_ref[0, i, 0]
        last_ref[0, i] = new_ref[0, i, width - 1]
    wall = jnp.zeros((8, depth), jnp.float32)
    row = lax.broadcasted_iota(jnp.int32, (8, depth), 0)
    for x in range(width):
        low = [new_ref[0, i, x, 0:8, :] for i in range(3)]
        high = [new_ref[0, i, x, rows - 8:rows, :] for i in range(3)]
        wall = wall + jnp.where(row == 7, spring_of(high) * (high[0] * high[1]), 0.0)
        wall = wall - jnp.where(row == 0, spring_of(low) * (low[0] * low[1]), 0.0)
    wall_ref[...] += wall * (0.5 / total_fields)


def second_fields(config, before, after, flow, noise, total_fields):
    fields, _, width, rows, depth = config.shape
    rim = jax.ShapeDtypeStruct((fields, 3, rows, depth), jnp.float32)
    wall = jax.ShapeDtypeStruct((8, depth), jnp.float32)
    return pl.pallas_call(
        functools.partial(second_kernel, total_fields),
        grid=(fields,),
        out_shape=[jax.ShapeDtypeStruct(config.shape, jnp.float32), rim, rim, wall],
        in_specs=[
            field_block(config.shape), rim_block(before.shape), rim_block(after.shape), whole_block(flow.shape),
            rim_block(before.shape, fields), rim_block(after.shape, fields), field_block(noise.shape),
        ],
        out_specs=[field_block(config.shape), rim_block(rim.shape), rim_block(rim.shape), whole_block(wall.shape)],
        scratch_shapes=[pltpu.VMEM((width, 12, rows, depth), jnp.float32)],
        compiler_params=params(),
        name="second_fields",
    )(config, before, after, flow, before, after, noise)


def flow_step(at, div_at, width, write):
    half = 0.5 * time_step
    for x in range(width):
        adv = [half * at(j, x) for j in range(3)]
        for i in range(3):
            here = at(i, x)
            below, above = at(i, x - 1), at(i, x + 1)
            left, right = down_y(here), up_y(here)
            back, front = down_z(here), up_z(here)
            along = adv[0] * (above - below) + adv[1] * (right - left) + adv[2] * (front - back)
            lap = (above + below) + (right + left) + (front + back) - 6.0 * here
            write(i, x, here - along + (time_step * viscosity) * lap + (time_step * stress_coef) * div_at(i, x))


def gather_parts(parts, div_ref):
    place = quad_place()
    for n, part in enumerate(parts):
        at = lax.rem(place + 4 - n, 4)
        rows = div_ref.shape[2]
        for i in range(3):
            div_ref[at, i] = part[i * rows:(i + 1) * rows]


def third_kernel(flow_ref, fbefore_ref, fafter_ref, p0, p1, p2, p3, start_ref, first_ref, last_ref, sums_ref, div_ref, wall_ref):
    _, width, rows, depth = flow_ref.shape
    gather_parts((p0, p1, p2, p3), div_ref)
    place = quad_place()
    for n, part in enumerate((p0, p1, p2, p3)):
        wall_ref[lax.rem(place + 4 - n, 4)] = part[3 * rows:]

    def at(i, x):
        if x < 0:
            return fbefore_ref[0, i]
        if x >= width:
            return fafter_ref[0, i]
        return flow_ref[i, x]

    def write(i, x, value):
        start_ref[i, x] = value

    flow_step(at, lambda i, x: div_ref[x, i], width, write)
    total = jnp.zeros((8, depth), jnp.float32)
    bend = jnp.zeros((8, depth), jnp.float32)
    edge = jnp.zeros((1, depth), jnp.float32)
    gain = jnp.zeros((1, depth), jnp.float32)
    for x in range(width):
        s, v, w = start_ref[0, x], start_ref[1, x], start_ref[2, x]
        term = v * (0.5 * (up_y(s) - down_y(s))) + w * (0.5 * (up_z(s) - down_z(s)))
        for r in range(rows // 8):
            total = total + s[8 * r:8 * r + 8]
            bend = bend + term[8 * r:8 * r + 8]
        edge = edge + (s[0:1] + s[rows - 1:rows])
        gain = gain + (v[0:1] - v[rows - 1:rows])
    row = lax.broadcasted_iota(jnp.int32, (8, depth), 0)
    sums = [
        jnp.sum(total, axis=0, keepdims=True),
        jnp.sum(bend, axis=0, keepdims=True) + viscosity * edge,
        0.5 * gain,
        jnp.sum((wall_ref[0] + wall_ref[1]) + (wall_ref[2] + wall_ref[3]), axis=0, keepdims=True),
    ]
    tile = jnp.zeros((8, depth), jnp.float32)
    for n, value in enumerate(sums):
        tile = jnp.where(row == n, value, tile)
    for n in range(sums_ref.shape[0]):
        sums_ref[n] = tile
    for i in range(3):
        first_ref[i] = start_ref[i, 0]
        last_ref[i] = start_ref[i, width - 1]


def third_flow(flow, left, right, parts, slabs):
    _, width, rows, depth = flow.shape
    end = jax.ShapeDtypeStruct((3, rows, depth), jnp.float32)
    sums = jax.ShapeDtypeStruct((slabs, 8, depth), jnp.float32)
    at = left.shape[0] - 1
    return pl.pallas_call(
        third_kernel,
        grid=(1,),
        out_shape=[jax.ShapeDtypeStruct(flow.shape, jnp.float32), end, end, sums],
        in_specs=[whole_block(flow.shape), rim_block(left.shape, at), rim_block(right.shape, at)]
        + [whole_block(parts[0].shape)] * 4,
        out_specs=[whole_block(flow.shape), whole_block(end.shape), whole_block(end.shape), whole_block(sums.shape)],
        scratch_shapes=[pltpu.VMEM((width, 3, rows, depth), jnp.float32), pltpu.VMEM((4, 8, depth), jnp.float32)],
        compiler_params=params(),
        name="third_flow",
    )(flow, left, right, *parts)


def lifts_of(shared_ref, walls, cells):
    sums = jnp.sum(jnp.sum(shared_ref[...], axis=0), axis=1, keepdims=True)
    lift = bulk_target - sums[0:1] / cells
    change = time_step * (stress_coef * sums[3:4] - sums[1:2] - lift * (sums[2:3] + 2.0 * viscosity * walls))
    return lift, -change / cells


def fourth_kernel(walls, cells, config_ref, before_ref, after_ref, start_ref, sbefore_ref, safter_ref, noise_ref, shared_ref, new_ref, slope_ref):
    width = config_ref.shape[2]

    def flow_at(i, x):
        if x < 0:
            return sbefore_ref[i]
        if x >= width:
            return safter_ref[i]
        return start_ref[i, x]

    @pl.when(pl.program_id(0) == 0)
    def _():
        lift = lifts_of(shared_ref, walls, cells)[0]
        fill_slopes(lambda i, x: flow_at(i, x) + lift if i == 0 else flow_at(i, x), slope_ref, width)

    advance_field(config_ref, before_ref, after_ref, noise_ref, new_ref, slope_ref)


def fourth_fields(config, before, after, start, sbefore, safter, noise, shared, walls, cells):
    fields, _, width, rows, depth = config.shape
    return pl.pallas_call(
        functools.partial(fourth_kernel, walls, cells),
        grid=(fields,),
        out_shape=jax.ShapeDtypeStruct(config.shape, jnp.float32),
        in_specs=[
            field_block(config.shape), rim_block(before.shape), rim_block(after.shape), whole_block(start.shape),
            whole_block(sbefore.shape), whole_block(safter.shape), field_block(noise.shape), whole_block(shared.shape),
        ],
        out_specs=field_block(config.shape),
        scratch_shapes=[pltpu.VMEM((width, 12, rows, depth), jnp.float32)],
        compiler_params=params(),
        name="fourth_fields",
    )(config, before, after, start, sbefore, safter, noise, shared)


def fifth_kernel(walls, cells, start_ref, sbefore_ref, safter_ref, p0, p1, p2, p3, shared_ref, out_ref, div_ref):
    width = start_ref.shape[1]
    lift, last_lift = lifts_of(shared_ref, walls, cells)
    gather_parts((p0, p1, p2, p3), div_ref)

    def at(i, x):
        if x < 0:
            value = sbefore_ref[i]
        elif x >= width:
            value = safter_ref[i]
        else:
            value = start_ref[i, x]
        return value + lift if i == 0 else value

    def write(i, x, value):
        out_ref[i, x] = value + last_lift if i == 0 else value

    flow_step(at, lambda i, x: div_ref[x, i], width, write)


def fifth_flow(start, sbefore, safter, parts, shared, walls, cells):
    _, width, rows, depth = start.shape
    return pl.pallas_call(
        functools.partial(fifth_kernel, walls, cells),
        grid=(1,),
        out_shape=jax.ShapeDtypeStruct(start.shape, jnp.float32),
        in_specs=[whole_block(start.shape)] + [whole_block(sbefore.shape)] * 2 + [whole_block(parts[0].shape)] * 4 + [whole_block(shared.shape)],
        out_specs=whole_block(start.shape),
        scratch_shapes=[pltpu.VMEM((width, 3, rows, depth), jnp.float32)],
        compiler_params=params(),
        name="fifth_flow",
    )(start, sbefore, safter, *parts, shared)


def pack_kernel(first_ref, last_ref, ffirst_ref, flast_ref, head_ref, tail_ref):
    velocity = pl.program_id(0) == pl.num_programs(0) - 1

    @pl.when(velocity)
    def _():
        head_ref[0] = ffirst_ref[:, 0]
        tail_ref[0] = flast_ref[:, 0]

    @pl.when(jnp.logical_not(velocity))
    def _():
        head_ref[0] = first_ref[0, :, 0]
        tail_ref[0] = last_ref[0, :, 0]


def pack_ends(config, flow):
    fields, _, width, rows, depth = config.shape
    rim = jax.ShapeDtypeStruct((fields + 1, 3, rows, depth), jnp.float32)

    def layer(x):
        return pl.BlockSpec((1, 3, 1, rows, depth), lambda k: (jnp.minimum(k, fields - 1), 0, x, 0, 0))

    def flow_layer(x):
        return pl.BlockSpec((3, 1, rows, depth), lambda k: (0, x, 0, 0))

    return pl.pallas_call(
        pack_kernel,
        grid=(fields + 1,),
        out_shape=[rim, rim],
        in_specs=[layer(0), layer(width - 1), flow_layer(0), flow_layer(width - 1)],
        out_specs=[rim_block(rim.shape)] * 2,
        compiler_params=params(),
        name="pack_ends",
    )(config, config, flow, flow)


def from_left(value):
    count = lax.axis_size("gx")
    return lax.ppermute(value, "gx", [(i, (i + 1) % count) for i in range(count)])


def from_right(value):
    count = lax.axis_size("gx")
    return lax.ppermute(value, "gx", [((i + 1) % count, i) for i in range(count)])


def quad_shift(value, by):
    count = lax.axis_size("row")
    return lax.ppermute(value, "row", [(i, i - i % 4 + (i + by) % 4) for i in range(count)])


def pair_swap(value, bit):
    count = lax.axis_size("row")
    return lax.ppermute(value, "row", [(i, i ^ bit) for i in range(count)])


def in_hbm(value):
    return pltpu.with_memory_space_constraint(value, pltpu.HBM)


def flat(value):
    return value.reshape(-1, value.shape[-1])


def after(value, *others):
    return lax.optimization_barrier((value,) + others)[0]


def shards(config, flow, keys):
    fields, _, width, rows, depth = config.shape
    total_fields = fields * lax.axis_size("row")
    slabs = lax.axis_size("gx")
    total_x = width * slabs
    cells = total_x * rows * depth

    keys = keys.reshape(-1)

    head, tail = pack_ends(in_hbm(config), in_hbm(flow))
    left, right = from_left(tail), from_right(head)
    noise = draw_noise(keys, 0, total_x, config.shape)
    inner = inner_stress(after(config, noise), total_fields)
    left, right = after(left, inner), after(right, inner)

    parts = stress_parts(inner, left, right, fields, total_fields)
    got = [quad_shift(parts[n], n) for n in (1, 2, 3)]
    config, first, last, wall = second_fields(config, after(left, parts[0]), right, flow, noise, total_fields)
    before, behind = from_left(last), from_right(first)
    got = [after(g, config) for g in got]
    own = jnp.concatenate([flat(parts[0] + got[0] + got[1] + got[2]), wall], axis=0)
    swap = pair_swap(own, 4)
    later = draw_noise(after(keys, own), 1, total_x, config.shape)
    inner = inner_stress(after(config, later), total_fields)
    own = own + after(swap, inner)
    div = [own] + [quad_shift(own, n) for n in (1, 2, 3)]

    parts = stress_parts(inner, after(before, own), behind, fields, total_fields)
    got = [quad_shift(parts[n], n) for n in (1, 2, 3)]

    start, first, last, sums = third_flow(flow, left, right, [after(d, parts[0]) for d in div], slabs)
    sleft, sright = from_left(last), from_right(first)
    shared = lax.all_to_all(sums, "gx", 0, 0)
    own = flat(parts[0] + got[0] + got[1] + after(got[2], start))
    own = own + pair_swap(own, 4)
    next_div = [own, quad_shift(after(own, shared), 1), quad_shift(own, 2), quad_shift(own, 3)]

    walls = total_x * depth
    config = fourth_fields(in_hbm(config), in_hbm(before), in_hbm(behind), in_hbm(start), sleft, sright, in_hbm(later), shared, walls, cells)
    flow = fifth_flow(start, sleft, sright, [after(d, config) for d in next_div], shared, walls, cells)
    return config, flow


def solution(mesh):
    placed = (P("row", None, "gx", None, None), P(None, "gx", None, None), P("row", None))
    return jax.shard_map(
        shards,
        mesh=mesh,
        in_specs=placed,
        out_specs=(P("row", None, "gx", None, None), P(None, "gx", None, None)),
        check_vma=False,
    )
```

```python
import functools
import math

import jax
import jax.numpy as jnp
from jax import lax
from jax.experimental import pallas as pl
from jax.experimental.pallas import tpu as pltpu
from jax.sharding import PartitionSpec as P

time_step = 0.05
viscosity = 0.5
stress_coef = 4.0
relax_time = 0.5
spring_limit = 10.0
spring_floor = 0.2
bulk_target = 1.0

SINE = (4.442882834149242, -7.308241154509167, 3.6062889576892747, -0.8457635932838079, 0.10920574854431932)
PAIRS = ((0, 0), (0, 1), (0, 2), (1, 1), (1, 2), (2, 2))
PLACE = ((0, 1, 2), (1, 3, 4), (2, 4, 5))
VMEM_LIMIT = 20 * 1024 * 1024
SMEM = pl.BlockSpec(memory_space=pltpu.SMEM)


def params():
    return pltpu.CompilerParams(vmem_limit_bytes=VMEM_LIMIT)


def mix_bits(value):
    value = value ^ lax.shift_right_logical(value, jnp.int32(16))
    value = value * jnp.int32(73244475)
    value = value ^ lax.shift_right_logical(value, jnp.int32(16))
    value = value * jnp.int32(73244475)
    return value ^ lax.shift_right_logical(value, jnp.int32(16))


def noise_of(salted, even):
    mask = jnp.int32(16777215)
    first = mix_bits(even ^ salted)
    second = mix_bits(even ^ (salted ^ 1))
    upper = ((first & mask).astype(jnp.float32) + 0.5) * (1.0 / 16777216.0)
    turn = (second & mask).astype(jnp.float32) * (1.0 / 16777216.0) + (0.5 / 16777216.0 - 0.5)
    square = jnp.maximum(jnp.log(upper) * (-2.0 * time_step / relax_time), 1e-30)
    radius = square * lax.rsqrt(square)
    w = turn * turn
    q = jnp.float32(SINE[4])
    for coef in SINE[3::-1]:
        q = q * w + coef
    q = q * turn
    return radius * (q * q - 1.0)


def noise_kernel(step, total_x, keys_ref, out_ref):
    _, _, width, rows, depth = out_ref.shape
    x_start = lax.axis_index("gx") * width
    salted = mix_bits(keys_ref[2 * pl.program_id(0) + step] + jnp.int32(40503))
    ypos = lax.broadcasted_iota(jnp.int32, (rows, depth), 0)
    zpos = lax.broadcasted_iota(jnp.int32, (rows, depth), 1)
    local = (ypos * depth + zpos) * 2

    def body(n, carry):
        comp = n // width
        x = n - comp * width
        even = local + ((comp * total_x + x_start + x) * rows) * (2 * depth)
        out_ref[0, comp, x] = noise_of(salted, even)
        return carry

    lax.fori_loop(0, 3 * width, body, 0)


def draw_noise(keys, step, total_x, shape):
    fields, comps, width, rows, depth = shape
    return pl.pallas_call(
        functools.partial(noise_kernel, step, total_x),
        grid=(fields,),
        out_shape=pltpu.HBM(shape, jnp.float32) if step else jax.ShapeDtypeStruct(shape, jnp.float32),
        in_specs=[SMEM],
        out_specs=pl.BlockSpec((1, comps, width, rows, depth), lambda k: (k, 0, 0, 0, 0)),
        compiler_params=params(),
        name="draw_noise",
    )(keys)


def up_z(f):
    return pltpu.roll(f, f.shape[-1] - 1, f.ndim - 1)


def down_z(f):
    return pltpu.roll(f, 1, f.ndim - 1)


def up_y(f):
    row = lax.broadcasted_iota(jnp.int32, f.shape, 0)
    return jnp.where(row == f.shape[0] - 1, 0.0, pltpu.roll(f, f.shape[0] - 1, 0))


def down_y(f):
    row = lax.broadcasted_iota(jnp.int32, f.shape, 0)
    return jnp.where(row == 0, 0.0, pltpu.roll(f, 1, 0))


def spring_of(q):
    length = q[0] * q[0] + q[1] * q[1] + q[2] * q[2]
    return 1.0 / jnp.maximum(1.0 - length * (1.0 / spring_limit), spring_floor)


def field_block(shape):
    return pl.BlockSpec((1,) + shape[1:], lambda k: (k,) + (0,) * (len(shape) - 1))


def whole_block(shape):
    return pl.BlockSpec(shape, lambda k: (0,) * len(shape))


def rim_block(shape, at=None):
    if at is None:
        return pl.BlockSpec((1,) + shape[1:], lambda k: (k, 0, 0, 0))
    return pl.BlockSpec((1,) + shape[1:], lambda k: (at, 0, 0, 0))


def quad_place():
    return lax.rem(lax.axis_index("row"), 4)


def inner_kernel(total_fields, config_ref, stress_ref):
    k = pl.program_id(0)

    def add(first):
        for x in range(config_ref.shape[2]):
            q = [config_ref[0, i, x] for i in range(3)]
            spring = spring_of(q) * (0.5 / total_fields)
            weighted = [spring * q[i] for i in range(3)]
            for p, (i, j) in enumerate(PAIRS):
                term = weighted[i] * q[j]
                stress_ref[p, x] = term if first else stress_ref[p, x] + term

    @pl.when(k == 0)
    def _():
        add(True)

    @pl.when(k > 0)
    def _():
        add(False)


def inner_stress(config, total_fields):
    fields, _, width, rows, depth = config.shape
    stress = jax.ShapeDtypeStruct((6, width, rows, depth), jnp.float32)
    return pl.pallas_call(
        functools.partial(inner_kernel, total_fields),
        grid=(fields,),
        out_shape=stress,
        in_specs=[field_block(config.shape)],
        out_specs=whole_block(stress.shape),
        compiler_params=params(),
        name="inner_stress",
    )(config)


def parts_kernel(total_fields, fields, stress_ref, before_ref, after_ref, *refs):
    outs, rim_ref = refs[:4], refs[4]
    width = stress_ref.shape[1]
    for side, ref in enumerate((before_ref, after_ref)):
        totals = None
        for k in range(fields):
            q = [ref[k, i] for i in range(3)]
            weighted = spring_of(q) * (0.5 / total_fields) * q[0]
            terms = [weighted * q[i] for i in range(3)]
            totals = terms if k == 0 else [t + u for t, u in zip(totals, terms)]
        for i in range(3):
            rim_ref[(width + 1) * side, i] = totals[i]
    for x in range(width):
        for i in range(3):
            rim_ref[x + 1, i] = stress_ref[PLACE[i][0], x]
    place = quad_place()
    for n, out in enumerate(outs):
        x = lax.rem(place + n, 4)
        for i in range(3):
            sy = stress_ref[PLACE[i][1], x]
            sz = stress_ref[PLACE[i][2], x]
            out[i] = (rim_ref[x + 2, i] - rim_ref[x, i]) + (up_y(sy) - down_y(sy)) + (up_z(sz) - down_z(sz))


def stress_parts(stress, before, after, fields, total_fields):
    _, width, rows, depth = stress.shape
    part = jax.ShapeDtypeStruct((3, rows, depth), jnp.float32)
    rim = (fields,) + before.shape[1:]
    return pl.pallas_call(
        functools.partial(parts_kernel, total_fields, fields),
        grid=(1,),
        out_shape=[part] * 4,
        in_specs=[whole_block(stress.shape), whole_block(rim), whole_block(rim)],
        out_specs=[whole_block(part.shape)] * 4,
        scratch_shapes=[pltpu.VMEM((width + 2, 3, rows, depth), jnp.float32)],
        compiler_params=params(),
        name="stress_parts",
    )(stress, before, after)


def fill_slopes(flow_at, slope_ref, width):
    half = 0.5 * time_step
    for x in range(width):
        for i in range(3):
            here = flow_at(i, x)
            slope_ref[x, 3 * i] = half * (flow_at(i, x + 1) - flow_at(i, x - 1))
            slope_ref[x, 3 * i + 1] = half * (up_y(here) - down_y(here))
            slope_ref[x, 3 * i + 2] = half * (up_z(here) - down_z(here))
            slope_ref[x, 9 + i] = half * here


def advance_field(config_ref, before_ref, after_ref, noise_ref, new_ref, slope_ref):
    _, _, width, rows, depth = config_ref.shape
    for x in range(width):
        q = [config_ref[0, i, x] for i in range(3)]
        keep = 1.0 - (time_step / (2.0 * relax_time)) * spring_of(q)
        for i in range(3):
            below = config_ref[0, i, x - 1] if x > 0 else before_ref[0, i]
            above = config_ref[0, i, x + 1] if x + 1 < width else after_ref[0, i]
            along = slope_ref[x, 9] * (above - below)
            along = along + slope_ref[x, 10] * (up_y(q[i]) - down_y(q[i]))
            along = along + slope_ref[x, 11] * (up_z(q[i]) - down_z(q[i]))
            stretch = slope_ref[x, 3 * i] * q[0] + slope_ref[x, 3 * i + 1] * q[1] + slope_ref[x, 3 * i + 2] * q[2]
            new_ref[0, i, x] = q[i] * keep + (stretch - along) + noise_ref[0, i, x]


def second_kernel(
    total_fields, config_ref, before_ref, after_ref, flow_ref, fbefore_ref, fafter_ref, noise_ref,
    new_ref, first_ref, last_ref, wall_ref, slope_ref,
):
    k = pl.program_id(0)
    _, _, width, rows, depth = config_ref.shape

    def flow_at(i, x):
        if x < 0:
            return fbefore_ref[0, i]
        if x >= width:
            return fafter_ref[0, i]
        return flow_ref[i, x]

    @pl.when(k == 0)
    def _():
        fill_slopes(flow_at, slope_ref, width)
        wall_ref[...] = jnp.zeros_like(wall_ref)

    advance_field(config_ref, before_ref, after_ref, noise_ref, new_ref, slope_ref)
    for i in range(3):
        first_ref[0, i] = new_ref[0, i, 0]
        last_ref[0, i] = new_ref[0, i, width - 1]
    wall = jnp.zeros((8, depth), jnp.float32)
    row = lax.broadcasted_iota(jnp.int32, (8, depth), 0)
    for x in range(width):
        low = [new_ref[0, i, x, 0:8, :] for i in range(3)]
        high = [new_ref[0, i, x, rows - 8:rows, :] for i in range(3)]
        wall = wall + jnp.where(row == 7, spring_of(high) * (high[0] * high[1]), 0.0)
        wall = wall - jnp.where(row == 0, spring_of(low) * (low[0] * low[1]), 0.0)
    wall_ref[...] += wall * (0.5 / total_fields)


def second_fields(config, before, after, flow, noise, total_fields):
    fields, _, width, rows, depth = config.shape
    rim = jax.ShapeDtypeStruct((fields, 3, rows, depth), jnp.float32)
    wall = jax.ShapeDtypeStruct((8, depth), jnp.float32)
    return pl.pallas_call(
        functools.partial(second_kernel, total_fields),
        grid=(fields,),
        out_shape=[jax.ShapeDtypeStruct(config.shape, jnp.float32), rim, rim, wall],
        in_specs=[
            field_block(config.shape), rim_block(before.shape), rim_block(after.shape), whole_block(flow.shape),
            rim_block(before.shape, fields), rim_block(after.shape, fields), field_block(noise.shape),
        ],
        out_specs=[field_block(config.shape), rim_block(rim.shape), rim_block(rim.shape), whole_block(wall.shape)],
        scratch_shapes=[pltpu.VMEM((width, 12, rows, depth), jnp.float32)],
        compiler_params=params(),
        name="second_fields",
    )(config, before, after, flow, before, after, noise)


def flow_step(at, div_at, width, write):
    half = 0.5 * time_step
    for x in range(width):
        adv = [half * at(j, x) for j in range(3)]
        for i in range(3):
            here = at(i, x)
            below, above = at(i, x - 1), at(i, x + 1)
            left, right = down_y(here), up_y(here)
            back, front = down_z(here), up_z(here)
            along = adv[0] * (above - below) + adv[1] * (right - left) + adv[2] * (front - back)
            lap = (above + below) + (right + left) + (front + back) - 6.0 * here
            write(i, x, here - along + (time_step * viscosity) * lap + (time_step * stress_coef) * div_at(i, x))


def gather_parts(parts, div_ref):
    place = quad_place()
    for n, part in enumerate(parts):
        at = lax.rem(place + 4 - n, 4)
        rows = div_ref.shape[2]
        for i in range(3):
            div_ref[at, i] = part[i * rows:(i + 1) * rows]


def third_kernel(flow_ref, fbefore_ref, fafter_ref, p0, p1, p2, p3, start_ref, first_ref, last_ref, sums_ref, div_ref, wall_ref):
    _, width, rows, depth = flow_ref.shape
    gather_parts((p0, p1, p2, p3), div_ref)
    place = quad_place()
    for n, part in enumerate((p0, p1, p2, p3)):
        wall_ref[lax.rem(place + 4 - n, 4)] = part[3 * rows:]

    def at(i, x):
        if x < 0:
            return fbefore_ref[0, i]
        if x >= width:
            return fafter_ref[0, i]
        return flow_ref[i, x]

    def write(i, x, value):
        start_ref[i, x] = value

    flow_step(at, lambda i, x: div_ref[x, i], width, write)
    total = jnp.zeros((8, depth), jnp.float32)
    bend = jnp.zeros((8, depth), jnp.float32)
    edge = jnp.zeros((1, depth), jnp.float32)
    gain = jnp.zeros((1, depth), jnp.float32)
    for x in range(width):
        s, v, w = start_ref[0, x], start_ref[1, x], start_ref[2, x]
        term = v * (0.5 * (up_y(s) - down_y(s))) + w * (0.5 * (up_z(s) - down_z(s)))
        for r in range(rows // 8):
            total = total + s[8 * r:8 * r + 8]
            bend = bend + term[8 * r:8 * r + 8]
        edge = edge + (s[0:1] + s[rows - 1:rows])
        gain = gain + (v[0:1] - v[rows - 1:rows])
    lane = lax.broadcasted_iota(jnp.int32, (1, depth), 1)
    sums = [
        jnp.sum(total, axis=0, keepdims=True),
        jnp.sum(bend, axis=0, keepdims=True) + viscosity * edge,
        0.5 * gain,
        jnp.sum((wall_ref[0] + wall_ref[1]) + (wall_ref[2] + wall_ref[3]), axis=0, keepdims=True),
    ]
    tile = jnp.zeros((1, depth), jnp.float32)
    for n, value in enumerate(sums):
        tile = jnp.where(lane == n, jnp.sum(value, axis=1, keepdims=True), tile)
    for n in range(sums_ref.shape[0]):
        sums_ref[n] = tile
    for i in range(3):
        first_ref[i] = start_ref[i, 0]
        last_ref[i] = start_ref[i, width - 1]


def third_flow(flow, left, right, parts, slabs):
    _, width, rows, depth = flow.shape
    end = jax.ShapeDtypeStruct((3, rows, depth), jnp.float32)
    sums = jax.ShapeDtypeStruct((slabs, 1, depth), jnp.float32)
    at = left.shape[0] - 1
    return pl.pallas_call(
        third_kernel,
        grid=(1,),
        out_shape=[jax.ShapeDtypeStruct(flow.shape, jnp.float32), end, end, sums],
        in_specs=[whole_block(flow.shape), rim_block(left.shape, at), rim_block(right.shape, at)]
        + [whole_block(parts[0].shape)] * 4,
        out_specs=[whole_block(flow.shape), whole_block(end.shape), whole_block(end.shape), whole_block(sums.shape)],
        scratch_shapes=[pltpu.VMEM((width, 3, rows, depth), jnp.float32), pltpu.VMEM((4, 8, depth), jnp.float32)],
        compiler_params=params(),
        name="third_flow",
    )(flow, left, right, *parts)


def lifts_of(shared_ref, walls, cells):
    row = jnp.sum(shared_ref[...], axis=0)
    lane = lax.broadcasted_iota(jnp.int32, row.shape, 1)
    flux, bend, gain, wall = [jnp.sum(jnp.where(lane == n, row, 0.0), axis=1, keepdims=True) for n in range(4)]
    lift = bulk_target - flux / cells
    change = time_step * (stress_coef * wall - bend - lift * (gain + 2.0 * viscosity * walls))
    return lift, -change / cells


def fourth_kernel(walls, cells, config_ref, before_ref, after_ref, start_ref, sbefore_ref, safter_ref, noise_ref, shared_ref, new_ref, slope_ref):
    width = config_ref.shape[2]

    def flow_at(i, x):
        if x < 0:
            return sbefore_ref[i]
        if x >= width:
            return safter_ref[i]
        return start_ref[i, x]

    @pl.when(pl.program_id(0) == 0)
    def _():
        lift = lifts_of(shared_ref, walls, cells)[0]
        fill_slopes(lambda i, x: flow_at(i, x) + lift if i == 0 else flow_at(i, x), slope_ref, width)

    advance_field(config_ref, before_ref, after_ref, noise_ref, new_ref, slope_ref)


def fourth_fields(config, before, after, start, sbefore, safter, noise, shared, walls, cells):
    fields, _, width, rows, depth = config.shape
    return pl.pallas_call(
        functools.partial(fourth_kernel, walls, cells),
        grid=(fields,),
        out_shape=jax.ShapeDtypeStruct(config.shape, jnp.float32),
        in_specs=[
            field_block(config.shape), rim_block(before.shape), rim_block(after.shape), whole_block(start.shape),
            whole_block(sbefore.shape), whole_block(safter.shape), field_block(noise.shape), whole_block(shared.shape),
        ],
        out_specs=field_block(config.shape),
        scratch_shapes=[pltpu.VMEM((width, 12, rows, depth), jnp.float32)],
        compiler_params=params(),
        name="fourth_fields",
    )(config, before, after, start, sbefore, safter, noise, shared)


def fifth_kernel(walls, cells, start_ref, sbefore_ref, safter_ref, p0, p1, p2, p3, shared_ref, out_ref, div_ref):
    width = start_ref.shape[1]
    lift, last_lift = lifts_of(shared_ref, walls, cells)
    gather_parts((p0, p1, p2, p3), div_ref)

    def at(i, x):
        if x < 0:
            value = sbefore_ref[i]
        elif x >= width:
            value = safter_ref[i]
        else:
            value = start_ref[i, x]
        return value + lift if i == 0 else value

    def write(i, x, value):
        out_ref[i, x] = value + last_lift if i == 0 else value

    flow_step(at, lambda i, x: div_ref[x, i], width, write)


def fifth_flow(start, sbefore, safter, parts, shared, walls, cells):
    _, width, rows, depth = start.shape
    return pl.pallas_call(
        functools.partial(fifth_kernel, walls, cells),
        grid=(1,),
        out_shape=jax.ShapeDtypeStruct(start.shape, jnp.float32),
        in_specs=[whole_block(start.shape)] + [whole_block(sbefore.shape)] * 2 + [whole_block(parts[0].shape)] * 4 + [whole_block(shared.shape)],
        out_specs=whole_block(start.shape),
        scratch_shapes=[pltpu.VMEM((width, 3, rows, depth), jnp.float32)],
        compiler_params=params(),
        name="fifth_flow",
    )(start, sbefore, safter, *parts, shared)


def pack_kernel(first_ref, last_ref, ffirst_ref, flast_ref, head_ref, tail_ref):
    fields = first_ref.shape[0]
    for k in range(fields):
        for i in range(3):
            head_ref[k, i] = first_ref[k, i, 0]
            tail_ref[k, i] = last_ref[k, i, 0]
    for i in range(3):
        head_ref[fields, i] = ffirst_ref[i, 0]
        tail_ref[fields, i] = flast_ref[i, 0]


def pack_ends(config, flow):
    fields, _, width, rows, depth = config.shape
    rim = jax.ShapeDtypeStruct((fields + 1, 3, rows, depth), jnp.float32)

    def layer(x):
        return pl.BlockSpec((fields, 3, 1, rows, depth), lambda k: (0, 0, x, 0, 0))

    def flow_layer(x):
        return pl.BlockSpec((3, 1, rows, depth), lambda k: (0, x, 0, 0))

    return pl.pallas_call(
        pack_kernel,
        grid=(1,),
        out_shape=[rim, rim],
        in_specs=[layer(0), layer(width - 1), flow_layer(0), flow_layer(width - 1)],
        out_specs=[whole_block(rim.shape)] * 2,
        compiler_params=params(),
        name="pack_ends",
    )(config, config, flow, flow)


def from_left(value):
    count = lax.axis_size("gx")
    return lax.ppermute(value, "gx", [(i, (i + 1) % count) for i in range(count)])


def from_right(value):
    count = lax.axis_size("gx")
    return lax.ppermute(value, "gx", [((i + 1) % count, i) for i in range(count)])


def quad_shift(value, by):
    count = lax.axis_size("row")
    return lax.ppermute(value, "row", [(i, i - i % 4 + (i + by) % 4) for i in range(count)])


def pair_swap(value, bit):
    count = lax.axis_size("row")
    return lax.ppermute(value, "row", [(i, i ^ bit) for i in range(count)])


def in_hbm(value):
    return pltpu.with_memory_space_constraint(value, pltpu.HBM)


def flat(value):
    return value.reshape(-1, value.shape[-1])


def after(value, *others):
    return lax.optimization_barrier((value,) + others)[0]


def shards(config, flow, keys):
    fields, _, width, rows, depth = config.shape
    total_fields = fields * lax.axis_size("row")
    slabs = lax.axis_size("gx")
    total_x = width * slabs
    cells = total_x * rows * depth

    keys = keys.reshape(-1)

    head, tail = pack_ends(in_hbm(config), in_hbm(flow))
    left, right = from_left(tail), from_right(head)
    noise = draw_noise(keys, 0, total_x, config.shape)
    inner = inner_stress(after(config, noise), total_fields)
    left, right = after(left, inner), after(right, inner)

    parts = stress_parts(inner, left, right, fields, total_fields)
    got = [quad_shift(parts[n], n) for n in (1, 2, 3)]
    config, first, last, wall = second_fields(config, after(left, parts[0]), right, flow, noise, total_fields)
    before, behind = from_left(last), from_right(first)
    got = [after(g, config) for g in got]
    own = jnp.concatenate([flat(parts[0] + got[0] + got[1] + got[2]), wall], axis=0)
    swap = pair_swap(own, 4)
    later = draw_noise(after(keys, own), 1, total_x, config.shape)
    inner = inner_stress(after(config, later), total_fields)
    own = own + after(swap, inner)
    div = [own] + [quad_shift(own, n) for n in (1, 2, 3)]

    parts = stress_parts(inner, after(before, own), behind, fields, total_fields)
    got = [quad_shift(parts[n], n) for n in (1, 2, 3)]

    start, first, last, sums = third_flow(flow, left, right, [after(d, parts[0]) for d in div], slabs)
    sleft, sright = from_left(last), from_right(first)
    shared = lax.all_to_all(sums, "gx", 0, 0)
    own = flat(parts[0] + got[0] + got[1] + after(got[2], start))
    own = own + pair_swap(own, 4)
    next_div = [own, quad_shift(after(own, shared), 1), quad_shift(own, 2), quad_shift(own, 3)]

    walls = total_x * depth
    config = fourth_fields(in_hbm(config), in_hbm(before), in_hbm(behind), in_hbm(start), sleft, sright, in_hbm(later), shared, walls, cells)
    flow = fifth_flow(start, sleft, sright, [after(d, config) for d in next_div], shared, walls, cells)
    return config, flow


def solution(mesh):
    placed = (P("row", None, "gx", None, None), P(None, "gx", None, None), P("row", None))
    return jax.shard_map(
        shards,
        mesh=mesh,
        in_specs=placed,
        out_specs=(P("row", None, "gx", None, None), P(None, "gx", None, None)),
        check_vma=False,
    )
```

```python
import functools
import math

import jax
import jax.numpy as jnp
from jax import lax
from jax.experimental import pallas as pl
from jax.experimental.pallas import tpu as pltpu
from jax.sharding import PartitionSpec as P

time_step = 0.05
viscosity = 0.5
stress_coef = 4.0
relax_time = 0.5
spring_limit = 10.0
spring_floor = 0.2
bulk_target = 1.0

SINE = (4.442882834149242, -7.308241154509167, 3.6062889576892747, -0.8457635932838079, 0.10920574854431932)
PAIRS = ((0, 0), (0, 1), (0, 2), (1, 1), (1, 2), (2, 2))
PLACE = ((0, 1, 2), (1, 3, 4), (2, 4, 5))
VMEM_LIMIT = 20 * 1024 * 1024
SMEM = pl.BlockSpec(memory_space=pltpu.SMEM)


def params():
    return pltpu.CompilerParams(vmem_limit_bytes=VMEM_LIMIT)


def mix_bits(value):
    value = value ^ lax.shift_right_logical(value, jnp.int32(16))
    value = value * jnp.int32(73244475)
    value = value ^ lax.shift_right_logical(value, jnp.int32(16))
    value = value * jnp.int32(73244475)
    return value ^ lax.shift_right_logical(value, jnp.int32(16))


def noise_of(salted, even):
    mask = jnp.int32(16777215)
    first = mix_bits(even ^ salted)
    second = mix_bits(even ^ (salted ^ 1))
    upper = ((first & mask).astype(jnp.float32) + 0.5) * (1.0 / 16777216.0)
    turn = (second & mask).astype(jnp.float32) * (1.0 / 16777216.0) + (0.5 / 16777216.0 - 0.5)
    square = jnp.maximum(jnp.log(upper) * (-2.0 * time_step / relax_time), 1e-30)
    radius = square * lax.rsqrt(square)
    w = turn * turn
    q = jnp.float32(SINE[4])
    for coef in SINE[3::-1]:
        q = q * w + coef
    q = q * turn
    return radius * (q * q - 1.0)


def noise_kernel(step, total_x, keys_ref, out_ref):
    _, _, width, rows, depth = out_ref.shape
    x_start = lax.axis_index("gx") * width
    salted = mix_bits(keys_ref[2 * pl.program_id(0) + step] + jnp.int32(40503))
    ypos = lax.broadcasted_iota(jnp.int32, (rows, depth), 0)
    zpos = lax.broadcasted_iota(jnp.int32, (rows, depth), 1)
    local = (ypos * depth + zpos) * 2

    def body(n, carry):
        comp = n // width
        x = n - comp * width
        even = local + ((comp * total_x + x_start + x) * rows) * (2 * depth)
        out_ref[0, comp, x] = noise_of(salted, even)
        return carry

    lax.fori_loop(0, 3 * width, body, 0)


def draw_noise(keys, step, total_x, shape):
    fields, comps, width, rows, depth = shape
    return pl.pallas_call(
        functools.partial(noise_kernel, step, total_x),
        grid=(fields,),
        out_shape=pltpu.HBM(shape, jnp.float32) if step else jax.ShapeDtypeStruct(shape, jnp.float32),
        in_specs=[SMEM],
        out_specs=pl.BlockSpec((1, comps, width, rows, depth), lambda k: (k, 0, 0, 0, 0)),
        compiler_params=params(),
        name="draw_noise",
    )(keys)


def up_z(f):
    return pltpu.roll(f, f.shape[-1] - 1, f.ndim - 1)


def down_z(f):
    return pltpu.roll(f, 1, f.ndim - 1)


def up_y(f):
    row = lax.broadcasted_iota(jnp.int32, f.shape, 0)
    return jnp.where(row == f.shape[0] - 1, 0.0, pltpu.roll(f, f.shape[0] - 1, 0))


def down_y(f):
    row = lax.broadcasted_iota(jnp.int32, f.shape, 0)
    return jnp.where(row == 0, 0.0, pltpu.roll(f, 1, 0))


def spring_of(q):
    length = q[0] * q[0] + q[1] * q[1] + q[2] * q[2]
    return 1.0 / jnp.maximum(1.0 - length * (1.0 / spring_limit), spring_floor)


def field_block(shape):
    return pl.BlockSpec((1,) + shape[1:], lambda k: (k,) + (0,) * (len(shape) - 1))


def whole_block(shape):
    return pl.BlockSpec(shape, lambda k: (0,) * len(shape))


def rim_block(shape, at=None):
    if at is None:
        return pl.BlockSpec((1,) + shape[1:], lambda k: (k, 0, 0, 0))
    return pl.BlockSpec((1,) + shape[1:], lambda k: (at, 0, 0, 0))


def quad_place():
    return lax.rem(lax.axis_index("row"), 4)


def inner_kernel(total_fields, config_ref, stress_ref):
    k = pl.program_id(0)

    def add(first):
        for x in range(config_ref.shape[2]):
            q = [config_ref[0, i, x] for i in range(3)]
            spring = spring_of(q) * (0.5 / total_fields)
            weighted = [spring * q[i] for i in range(3)]
            for p, (i, j) in enumerate(PAIRS):
                term = weighted[i] * q[j]
                stress_ref[p, x] = term if first else stress_ref[p, x] + term

    @pl.when(k == 0)
    def _():
        add(True)

    @pl.when(k > 0)
    def _():
        add(False)


def inner_stress(config, total_fields):
    fields, _, width, rows, depth = config.shape
    stress = jax.ShapeDtypeStruct((6, width, rows, depth), jnp.float32)
    return pl.pallas_call(
        functools.partial(inner_kernel, total_fields),
        grid=(fields,),
        out_shape=stress,
        in_specs=[field_block(config.shape)],
        out_specs=whole_block(stress.shape),
        compiler_params=params(),
        name="inner_stress",
    )(config)


def parts_kernel(total_fields, fields, stress_ref, before_ref, after_ref, *refs):
    outs, rim_ref = refs[:4], refs[4]
    width = stress_ref.shape[1]
    for side, ref in enumerate((before_ref, after_ref)):
        totals = None
        for k in range(fields):
            q = [ref[k, i] for i in range(3)]
            weighted = spring_of(q) * (0.5 / total_fields) * q[0]
            terms = [weighted * q[i] for i in range(3)]
            totals = terms if k == 0 else [t + u for t, u in zip(totals, terms)]
        for i in range(3):
            rim_ref[(width + 1) * side, i] = totals[i]
    for x in range(width):
        for i in range(3):
            rim_ref[x + 1, i] = stress_ref[PLACE[i][0], x]
    place = quad_place()
    for n, out in enumerate(outs):
        x = lax.rem(place + n, 4)
        for i in range(3):
            sy = stress_ref[PLACE[i][1], x]
            sz = stress_ref[PLACE[i][2], x]
            out[i] = (rim_ref[x + 2, i] - rim_ref[x, i]) + (up_y(sy) - down_y(sy)) + (up_z(sz) - down_z(sz))


def stress_parts(stress, before, after, fields, total_fields):
    _, width, rows, depth = stress.shape
    part = jax.ShapeDtypeStruct((3, rows, depth), jnp.float32)
    rim = (fields,) + before.shape[1:]
    return pl.pallas_call(
        functools.partial(parts_kernel, total_fields, fields),
        grid=(1,),
        out_shape=[part] * 4,
        in_specs=[whole_block(stress.shape), whole_block(rim), whole_block(rim)],
        out_specs=[whole_block(part.shape)] * 4,
        scratch_shapes=[pltpu.VMEM((width + 2, 3, rows, depth), jnp.float32)],
        compiler_params=params(),
        name="stress_parts",
    )(stress, before, after)


def fill_slopes(flow_at, slope_ref, width):
    half = 0.5 * time_step
    for x in range(width):
        for i in range(3):
            here = flow_at(i, x)
            slope_ref[x, 3 * i] = half * (flow_at(i, x + 1) - flow_at(i, x - 1))
            slope_ref[x, 3 * i + 1] = half * (up_y(here) - down_y(here))
            slope_ref[x, 3 * i + 2] = half * (up_z(here) - down_z(here))
            slope_ref[x, 9 + i] = half * here


def advance_field(config_ref, before_ref, after_ref, noise_ref, new_ref, slope_ref):
    _, _, width, rows, depth = config_ref.shape
    for x in range(width):
        q = [config_ref[0, i, x] for i in range(3)]
        keep = 1.0 - (time_step / (2.0 * relax_time)) * spring_of(q)
        for i in range(3):
            below = config_ref[0, i, x - 1] if x > 0 else before_ref[0, i]
            above = config_ref[0, i, x + 1] if x + 1 < width else after_ref[0, i]
            along = slope_ref[x, 9] * (above - below)
            along = along + slope_ref[x, 10] * (up_y(q[i]) - down_y(q[i]))
            along = along + slope_ref[x, 11] * (up_z(q[i]) - down_z(q[i]))
            stretch = slope_ref[x, 3 * i] * q[0] + slope_ref[x, 3 * i + 1] * q[1] + slope_ref[x, 3 * i + 2] * q[2]
            new_ref[0, i, x] = q[i] * keep + (stretch - along) + noise_ref[0, i, x]


def second_kernel(
    total_fields, config_ref, before_ref, after_ref, flow_ref, fbefore_ref, fafter_ref, noise_ref,
    new_ref, first_ref, last_ref, wall_ref, slope_ref,
):
    k = pl.program_id(0)
    _, _, width, rows, depth = config_ref.shape

    def flow_at(i, x):
        if x < 0:
            return fbefore_ref[0, i]
        if x >= width:
            return fafter_ref[0, i]
        return flow_ref[i, x]

    @pl.when(k == 0)
    def _():
        fill_slopes(flow_at, slope_ref, width)
        wall_ref[...] = jnp.zeros_like(wall_ref)

    advance_field(config_ref, before_ref, after_ref, noise_ref, new_ref, slope_ref)
    for i in range(3):
        first_ref[0, i] = new_ref[0, i, 0]
        last_ref[0, i] = new_ref[0, i, width - 1]
    wall = jnp.zeros((8, depth), jnp.float32)
    row = lax.broadcasted_iota(jnp.int32, (8, depth), 0)
    for x in range(width):
        low = [new_ref[0, i, x, 0:8, :] for i in range(3)]
        high = [new_ref[0, i, x, rows - 8:rows, :] for i in range(3)]
        wall = wall + jnp.where(row == 7, spring_of(high) * (high[0] * high[1]), 0.0)
        wall = wall - jnp.where(row == 0, spring_of(low) * (low[0] * low[1]), 0.0)
    wall_ref[...] += wall * (0.5 / total_fields)


def second_fields(config, before, after, flow, noise, total_fields):
    fields, _, width, rows, depth = config.shape
    rim = jax.ShapeDtypeStruct((fields, 3, rows, depth), jnp.float32)
    wall = jax.ShapeDtypeStruct((8, depth), jnp.float32)
    return pl.pallas_call(
        functools.partial(second_kernel, total_fields),
        grid=(fields,),
        out_shape=[jax.ShapeDtypeStruct(config.shape, jnp.float32), rim, rim, wall],
        in_specs=[
            field_block(config.shape), rim_block(before.shape), rim_block(after.shape), whole_block(flow.shape),
            rim_block(before.shape, fields), rim_block(after.shape, fields), field_block(noise.shape),
        ],
        out_specs=[field_block(config.shape), rim_block(rim.shape), rim_block(rim.shape), whole_block(wall.shape)],
        scratch_shapes=[pltpu.VMEM((width, 12, rows, depth), jnp.float32)],
        compiler_params=params(),
        name="second_fields",
    )(config, before, after, flow, before, after, noise)


def flow_step(at, div_at, width, write):
    half = 0.5 * time_step
    for x in range(width):
        adv = [half * at(j, x) for j in range(3)]
        for i in range(3):
            here = at(i, x)
            below, above = at(i, x - 1), at(i, x + 1)
            left, right = down_y(here), up_y(here)
            back, front = down_z(here), up_z(here)
            along = adv[0] * (above - below) + adv[1] * (right - left) + adv[2] * (front - back)
            lap = (above + below) + (right + left) + (front + back) - 6.0 * here
            write(i, x, here - along + (time_step * viscosity) * lap + (time_step * stress_coef) * div_at(i, x))


def gather_parts(parts, div_ref):
    place = quad_place()
    for n, part in enumerate(parts):
        at = lax.rem(place + 4 - n, 4)
        rows = div_ref.shape[2]
        for i in range(3):
            div_ref[at, i] = part[i * rows:(i + 1) * rows]


def third_kernel(flow_ref, fbefore_ref, fafter_ref, p0, p1, p2, p3, start_ref, first_ref, last_ref, sums_ref, div_ref, wall_ref):
    _, width, rows, depth = flow_ref.shape
    gather_parts((p0, p1, p2, p3), div_ref)
    place = quad_place()
    for n, part in enumerate((p0, p1, p2, p3)):
        wall_ref[lax.rem(place + 4 - n, 4)] = part[3 * rows:]

    def at(i, x):
        if x < 0:
            return fbefore_ref[0, i]
        if x >= width:
            return fafter_ref[0, i]
        return flow_ref[i, x]

    def write(i, x, value):
        start_ref[i, x] = value

    flow_step(at, lambda i, x: div_ref[x, i], width, write)
    total = jnp.zeros((8, depth), jnp.float32)
    bend = jnp.zeros((8, depth), jnp.float32)
    edge = jnp.zeros((1, depth), jnp.float32)
    gain = jnp.zeros((1, depth), jnp.float32)
    for x in range(width):
        s, v, w = start_ref[0, x], start_ref[1, x], start_ref[2, x]
        term = v * (0.5 * (up_y(s) - down_y(s))) + w * (0.5 * (up_z(s) - down_z(s)))
        for r in range(rows // 8):
            total = total + s[8 * r:8 * r + 8]
            bend = bend + term[8 * r:8 * r + 8]
        edge = edge + (s[0:1] + s[rows - 1:rows])
        gain = gain + (v[0:1] - v[rows - 1:rows])
    lane = lax.broadcasted_iota(jnp.int32, (1, depth), 1)
    sums = [
        jnp.sum(total, axis=0, keepdims=True),
        jnp.sum(bend, axis=0, keepdims=True) + viscosity * edge,
        0.5 * gain,
        jnp.sum((wall_ref[0] + wall_ref[1]) + (wall_ref[2] + wall_ref[3]), axis=0, keepdims=True),
    ]
    tile = jnp.zeros((1, depth), jnp.float32)
    for n, value in enumerate(sums):
        tile = jnp.where(lane == n, jnp.sum(value, axis=1, keepdims=True), tile)
    for n in range(sums_ref.shape[0]):
        sums_ref[n] = tile
    for i in range(3):
        first_ref[i] = start_ref[i, 0]
        last_ref[i] = start_ref[i, width - 1]


def third_flow(flow, left, right, parts, slabs):
    _, width, rows, depth = flow.shape
    end = jax.ShapeDtypeStruct((3, rows, depth), jnp.float32)
    sums = jax.ShapeDtypeStruct((slabs, 1, depth), jnp.float32)
    at = left.shape[0] - 1
    return pl.pallas_call(
        third_kernel,
        grid=(1,),
        out_shape=[jax.ShapeDtypeStruct(flow.shape, jnp.float32), end, end, sums],
        in_specs=[whole_block(flow.shape), rim_block(left.shape, at), rim_block(right.shape, at)]
        + [whole_block(parts[0].shape)] * 4,
        out_specs=[whole_block(flow.shape), whole_block(end.shape), whole_block(end.shape), whole_block(sums.shape)],
        scratch_shapes=[pltpu.VMEM((width, 3, rows, depth), jnp.float32), pltpu.VMEM((4, 8, depth), jnp.float32)],
        compiler_params=params(),
        name="third_flow",
    )(flow, left, right, *parts)


def lifts_of(shared_ref, walls, cells):
    row = jnp.sum(shared_ref[...], axis=0)
    lane = lax.broadcasted_iota(jnp.int32, row.shape, 1)
    flux, bend, gain, wall = [jnp.sum(jnp.where(lane == n, row, 0.0), axis=1, keepdims=True) for n in range(4)]
    lift = bulk_target - flux / cells
    change = time_step * (stress_coef * wall - bend - lift * (gain + 2.0 * viscosity * walls))
    return lift, -change / cells


def fourth_kernel(config_ref, before_ref, after_ref, start_ref, sbefore_ref, safter_ref, noise_ref, new_ref, slope_ref):
    width = config_ref.shape[2]

    def flow_at(i, x):
        if x < 0:
            return sbefore_ref[i]
        if x >= width:
            return safter_ref[i]
        return start_ref[i, x]

    @pl.when(pl.program_id(0) == 0)
    def _():
        fill_slopes(flow_at, slope_ref, width)

    advance_field(config_ref, before_ref, after_ref, noise_ref, new_ref, slope_ref)


def fourth_fields(config, before, after, start, sbefore, safter, noise):
    fields, _, width, rows, depth = config.shape
    return pl.pallas_call(
        fourth_kernel,
        grid=(fields,),
        out_shape=jax.ShapeDtypeStruct(config.shape, jnp.float32),
        in_specs=[
            field_block(config.shape), rim_block(before.shape), rim_block(after.shape), whole_block(start.shape),
            whole_block(sbefore.shape), whole_block(safter.shape), field_block(noise.shape),
        ],
        out_specs=field_block(config.shape),
        scratch_shapes=[pltpu.VMEM((width, 12, rows, depth), jnp.float32)],
        compiler_params=params(),
        name="fourth_fields",
    )(config, before, after, start, sbefore, safter, noise)


def lift_kernel(walls, cells, rough_ref, config_ref, before_ref, after_ref, shared_ref, out_ref):
    _, _, width, rows, depth = config_ref.shape
    half = (0.5 * time_step) * lifts_of(shared_ref, walls, cells)[0]
    row = lax.broadcasted_iota(jnp.int32, (rows, depth), 0)
    slope = jnp.where(row == 0, half, jnp.where(row == rows - 1, -half, 0.0))
    for x in range(width):
        for i in range(3):
            below = config_ref[0, i, x - 1] if x > 0 else before_ref[0, i]
            above = config_ref[0, i, x + 1] if x + 1 < width else after_ref[0, i]
            value = rough_ref[0, i, x] - half * (above - below)
            out_ref[0, i, x] = value + slope * config_ref[0, 1, x] if i == 0 else value


def lift_fields(rough, config, before, after, shared, walls, cells):
    return pl.pallas_call(
        functools.partial(lift_kernel, walls, cells),
        grid=(config.shape[0],),
        out_shape=jax.ShapeDtypeStruct(config.shape, jnp.float32),
        in_specs=[
            field_block(config.shape), field_block(config.shape), rim_block(before.shape), rim_block(after.shape),
            whole_block(shared.shape),
        ],
        out_specs=field_block(config.shape),
        compiler_params=params(),
        name="lift_fields",
    )(rough, config, before, after, shared)


def fifth_kernel(walls, cells, start_ref, sbefore_ref, safter_ref, p0, p1, p2, p3, shared_ref, out_ref, div_ref):
    width = start_ref.shape[1]
    lift, last_lift = lifts_of(shared_ref, walls, cells)
    gather_parts((p0, p1, p2, p3), div_ref)

    def at(i, x):
        if x < 0:
            value = sbefore_ref[i]
        elif x >= width:
            value = safter_ref[i]
        else:
            value = start_ref[i, x]
        return value + lift if i == 0 else value

    def write(i, x, value):
        out_ref[i, x] = value + last_lift if i == 0 else value

    flow_step(at, lambda i, x: div_ref[x, i], width, write)


def fifth_flow(start, sbefore, safter, parts, shared, walls, cells):
    _, width, rows, depth = start.shape
    return pl.pallas_call(
        functools.partial(fifth_kernel, walls, cells),
        grid=(1,),
        out_shape=jax.ShapeDtypeStruct(start.shape, jnp.float32),
        in_specs=[whole_block(start.shape)] + [whole_block(sbefore.shape)] * 2 + [whole_block(parts[0].shape)] * 4 + [whole_block(shared.shape)],
        out_specs=whole_block(start.shape),
        scratch_shapes=[pltpu.VMEM((width, 3, rows, depth), jnp.float32)],
        compiler_params=params(),
        name="fifth_flow",
    )(start, sbefore, safter, *parts, shared)


def pack_kernel(first_ref, last_ref, ffirst_ref, flast_ref, head_ref, tail_ref):
    fields = first_ref.shape[0]
    for k in range(fields):
        for i in range(3):
            head_ref[k, i] = first_ref[k, i, 0]
            tail_ref[k, i] = last_ref[k, i, 0]
    for i in range(3):
        head_ref[fields, i] = ffirst_ref[i, 0]
        tail_ref[fields, i] = flast_ref[i, 0]


def pack_ends(config, flow):
    fields, _, width, rows, depth = config.shape
    rim = jax.ShapeDtypeStruct((fields + 1, 3, rows, depth), jnp.float32)

    def layer(x):
        return pl.BlockSpec((fields, 3, 1, rows, depth), lambda k: (0, 0, x, 0, 0))

    def flow_layer(x):
        return pl.BlockSpec((3, 1, rows, depth), lambda k: (0, x, 0, 0))

    return pl.pallas_call(
        pack_kernel,
        grid=(1,),
        out_shape=[rim, rim],
        in_specs=[layer(0), layer(width - 1), flow_layer(0), flow_layer(width - 1)],
        out_specs=[whole_block(rim.shape)] * 2,
        compiler_params=params(),
        name="pack_ends",
    )(config, config, flow, flow)


def from_left(value):
    count = lax.axis_size("gx")
    return lax.ppermute(value, "gx", [(i, (i + 1) % count) for i in range(count)])


def from_right(value):
    count = lax.axis_size("gx")
    return lax.ppermute(value, "gx", [((i + 1) % count, i) for i in range(count)])


def quad_shift(value, by):
    count = lax.axis_size("row")
    return lax.ppermute(value, "row", [(i, i - i % 4 + (i + by) % 4) for i in range(count)])


def pair_swap(value, bit):
    count = lax.axis_size("row")
    return lax.ppermute(value, "row", [(i, i ^ bit) for i in range(count)])


def in_hbm(value):
    return pltpu.with_memory_space_constraint(value, pltpu.HBM)


def flat(value):
    return value.reshape(-1, value.shape[-1])


def after(value, *others):
    return lax.optimization_barrier((value,) + others)[0]


def shards(config, flow, keys):
    fields, _, width, rows, depth = config.shape
    total_fields = fields * lax.axis_size("row")
    slabs = lax.axis_size("gx")
    total_x = width * slabs
    cells = total_x * rows * depth

    keys = keys.reshape(-1)

    head, tail = pack_ends(in_hbm(config), in_hbm(flow))
    left, right = from_left(tail), from_right(head)
    noise = draw_noise(keys, 0, total_x, config.shape)
    inner = inner_stress(after(config, noise), total_fields)
    left, right = after(left, inner), after(right, inner)

    parts = stress_parts(inner, left, right, fields, total_fields)
    got = [quad_shift(parts[n], n) for n in (1, 2, 3)]
    config, first, last, wall = second_fields(config, after(left, parts[0]), right, flow, noise, total_fields)
    before, behind = from_left(last), from_right(first)
    got = [after(g, config) for g in got]
    own = jnp.concatenate([flat(parts[0] + got[0] + got[1] + got[2]), wall], axis=0)
    swap = pair_swap(own, 4)
    later = draw_noise(after(keys, own), 1, total_x, config.shape)
    inner = inner_stress(after(config, later), total_fields)
    own = own + after(swap, inner)
    div = [own] + [quad_shift(own, n) for n in (1, 2, 3)]

    parts = stress_parts(inner, after(before, own), behind, fields, total_fields)
    got = [quad_shift(parts[n], n) for n in (1, 2, 3)]

    start, first, last, sums = third_flow(flow, left, right, [after(d, parts[0]) for d in div], slabs)
    sleft, sright = from_left(last), from_right(first)
    shared = lax.all_to_all(sums, "gx", 0, 0)
    own = flat(parts[0] + got[0] + got[1] + after(got[2], start))
    own = own + pair_swap(own, 4)
    next_div = [own] + [quad_shift(own, n) for n in (1, 2, 3)]
    rough = fourth_fields(
        in_hbm(config), in_hbm(before), in_hbm(behind), in_hbm(start), after(sleft, own), sright, in_hbm(later)
    )
    shared = after(shared, rough)

    walls = total_x * depth
    rolls = [after(d, rough) for d in next_div]
    config = lift_fields(rough, in_hbm(config), in_hbm(before), in_hbm(behind), shared, walls, cells)
    flow = fifth_flow(start, sleft, sright, [after(d, config) for d in rolls], shared, walls, cells)
    return config, flow


def solution(mesh):
    placed = (P("row", None, "gx", None, None), P(None, "gx", None, None), P("row", None))
    return jax.shard_map(
        shards,
        mesh=mesh,
        in_specs=placed,
        out_specs=(P("row", None, "gx", None, None), P(None, "gx", None, None)),
        check_vma=False,
    )
```
